32 devices in a mesh: group: 2 (over y), expert: 4 (over z), replica: 2 (over x), tensor: 2 (over core).
Axes of the slice: x: 2, y: 2, z: 4, core: 2. Of those that a mesh axis runs over, the one named last changes fastest.
Arguments:
- tokens: bfloat16 [4, 960, 1024], P(('group', 'replica'), 'expert'), parts along dimension 0, may hold values from -6 to 6
- out_grad: bfloat16 [4, 960, 1024], P(('group', 'replica'), 'expert'), parts along dimension 0, may hold values from -6 to 6
- expert_ids: int32 [4, 960, 8], P(('group', 'replica'), 'expert'), parts along dimension 0, may hold values from 0 to 127, as said below
- route_weight: float32 [4, 960, 8], P(('group', 'replica'), 'expert'), parts along dimension 0, may hold values from 0.05 to 0.5
- gate_proj: bfloat16 [4, 768, 1024], P('expert', 'tensor'), may hold values from -0.1875 to 0.1875
- up_proj: bfloat16 [4, 768, 1024], P('expert', 'tensor'), may hold values from -0.1875 to 0.1875
- down_proj: bfloat16 [4, 768, 1024], P('expert', 'tensor'), may hold values from -0.21875 to 0.21875
- fragment: int32 [2], P('group'), parts along dimension 0, may hold values from 0 to 3
Outputs:
- grad_gate: bfloat16 [4, 4, 768, 1024], P(('group', 'replica'), 'expert', 'tensor'), parts along dimension 0
- grad_up: bfloat16 [4, 4, 768, 1024], P(('group', 'replica'), 'expert', 'tensor'), parts along dimension 0
- grad_down: bfloat16 [4, 4, 768, 1024], P(('group', 'replica'), 'expert', 'tensor'), parts along dimension 0
- expert_load: float32 [4, 4], P(('group', 'replica'), 'expert'), parts along dimension 0
The draws below stay inside these ranges and needn't reach their ends.
There are 2 independent parts, one for each index of `group`. The reference program is written for one: setup_inputs(seed, part) draws one part's arguments, and reference() takes and returns one part's arrays. A program takes and returns all parts, laid end to end along the dimension named above; an argument that names none is the same for every part. Nothing has to cross between parts.
Inputs may be any that keep to these rules, and one draw needn't show every extreme that they name: `expert_ids`: each row names 8 different experts. Among the rows of one device (aligned blocks of 240 rows of a replica), each expert below 4 is named by at most 60 rows; in every draw one such expert is named by exactly 60 rows in every block.
All inputs are finite; a program needn't handle non-finite values.
Results may differ from the reference program's by a relative error of at most 0.0058.
Values may be sent and summed in bfloat16 or wider, within the bound.
No kernel may reach another device: no remote copies, remote signals or barrier semaphores. Data moves between devices by JAX's collectives and lax.ppermute only.
A program may use at most 64 MiB of HBM per device.

```python
import math
import jax
import jax.numpy as jnp
from jax import lax

D = 1024
FF = 768
EXPERTS = 128
TOP = 8
FRAGS = 4
TOK_DEV = 240
WIN = 4
TOK_REP = 960
CAP = 60
N_EXPERT = 4
N_REPLICA = 2


def draw_expert_ids(key, part):
    key = jax.random.fold_in(key, 7)
    keys = jax.random.split(key, 6)
    blocks = N_REPLICA * (TOK_REP // TOK_DEV)
    column = jnp.arange(WIN, dtype=jnp.int32)
    level = jax.random.randint(keys[0], (WIN,), 0, 4)
    hottest = jax.random.randint(keys[1], (), 0, WIN)
    level = jnp.where(column == hottest, 0, level)
    base = jnp.right_shift(jnp.full((WIN,), CAP, jnp.int32), level.astype(jnp.int32))
    jitter = jax.random.randint(keys[2], (blocks, WIN), 0, 1 << 20) % (base // 2 + 1)[None, :]
    wanted = jnp.where(column[None, :] == hottest, CAP, base[None, :] - jitter)
    scores = jax.random.randint(keys[3], (blocks, WIN, TOK_DEV), 0, 1 << 20) * TOK_DEV + jnp.arange(TOK_DEV, dtype=jnp.int32)
    ranks = jnp.argsort(jnp.argsort(scores, axis=2), axis=2)
    chosen = jnp.transpose(ranks < wanted[:, :, None], (0, 2, 1))
    order = (column - hottest) % WIN
    before = order[:, None] <= order[None, :]
    running = jnp.sum((chosen[:, :, :, None] & before[None, None, :, :]).astype(jnp.int32), axis=2)
    kept = chosen & (running <= TOP)
    slot_of = jnp.cumsum(kept.astype(jnp.int32), axis=2) - 1
    window_count = jnp.sum(kept.astype(jnp.int32), axis=2)
    others_count = EXPERTS - WIN
    scores_rest = jax.random.randint(keys[4], (blocks, TOK_DEV, others_count), 0, 1 << 20) * others_count + jnp.arange(others_count, dtype=jnp.int32)
    others = jnp.argsort(scores_rest, axis=2)[:, :, :TOP] + WIN
    places = jnp.arange(TOP, dtype=jnp.int32)
    from_window = jnp.sum(jnp.where(kept[:, :, None, :] & (slot_of[:, :, None, :] == places[None, None, :, None]), column[None, None, None, :], 0), axis=3)
    picks = jnp.clip(places[None, None, :] - window_count[:, :, None], 0, TOP - 1)
    from_others = jnp.take_along_axis(others, picks, axis=2)
    chosen_ids = jnp.where(places[None, None, :] < window_count[:, :, None], from_window, from_others)
    scores_mix = jax.random.randint(keys[5], (blocks, TOK_DEV, TOP), 0, 1 << 20) * TOP + places
    shuffle = jnp.argsort(scores_mix, axis=2)
    chosen_ids = jnp.take_along_axis(chosen_ids, shuffle, axis=2)
    return chosen_ids.reshape(N_REPLICA, TOK_REP, TOP).astype(jnp.int32)


def levels(stream_key, shape, shards, smallest, largest):
    gain, own = 1.0, jax.random.fold_in(stream_key, 6)
    for axis_at, blocks in shards:
        heights = jnp.exp(jax.random.uniform(jax.random.fold_in(own, axis_at), (blocks,), jnp.float32, smallest / len(shards), largest / len(shards)))
        gain = gain * jnp.repeat(heights, shape[axis_at] // blocks).reshape([-1 if axis == axis_at else 1 for axis in range(len(shape))])
    return gain


def noise(key, shape, spread, most, cuts=(), held_as=jnp.bfloat16):
    gain = levels(key, shape, cuts, -0.22, 0.18) if cuts else 1.0
    drawn = jax.random.normal(key, shape, jnp.float32) * spread * gain
    return jnp.minimum(jnp.maximum(drawn, -most), most).astype(held_as)


def setup_inputs(seed: int = 0, part: int = 0) -> dict:
    streams_of = jax.random.split(jax.random.key(seed), 9)
    part_splits = jax.random.split(jax.random.fold_in(streams_of[8], part), 9)
    tokens = noise(part_splits[0], (N_REPLICA, TOK_REP, D), 1.0, 6.0, ((0, 2), (1, 4)))
    out_grad = noise(part_splits[1], (N_REPLICA, TOK_REP, D), 1.0, 6.0, ((0, 2), (1, 4)))
    expert_ids = draw_expert_ids(jax.random.fold_in(jax.random.fold_in(streams_of[8], part), 71), part)
    route_weight = jnp.clip(jnp.exp(math.log(0.5) - 2.3025851 * jax.random.uniform(part_splits[3], (N_REPLICA, TOK_REP, TOP), jnp.float32) ** levels(part_splits[3], (N_REPLICA, TOK_REP, TOP), ((0, 2), (1, 4)), -0.2, 0.2)), 0.05, 0.5)
    gate_proj = noise(streams_of[4], (WIN, FF, D), D ** -0.5, 0.1875, ((0, 4), (1, 2)))
    up_proj = noise(streams_of[5], (WIN, FF, D), D ** -0.5, 0.1875, ((0, 4), (1, 2)))
    down_proj = noise(streams_of[6], (WIN, FF, D), FF ** -0.5, 0.21875, ((0, 4), (1, 2)))
    fragment = jax.random.randint(part_splits[7], (1,), 0, FRAGS).astype(jnp.int32)
    return dict(tokens=tokens, out_grad=out_grad, expert_ids=expert_ids, route_weight=route_weight, gate_proj=gate_proj, up_proj=up_proj, down_proj=down_proj, fragment=fragment)


def expert_terms(x_rows, q_rows, w_gate, w_up, w_down):
    gate_pre = jnp.dot(x_rows, w_gate.T, preferred_element_type=jnp.float32)
    up_pre = jnp.dot(x_rows, w_up.T, preferred_element_type=jnp.float32)
    gate_sig = jax.nn.sigmoid(gate_pre)
    gate_act = gate_pre * gate_sig
    hidden = (gate_act * up_pre).astype(jnp.bfloat16)
    hidden_grad = jnp.dot(q_rows, w_down.T, preferred_element_type=jnp.float32)
    gate_grad = (hidden_grad * up_pre * gate_sig * (1.0 + gate_pre * (1.0 - gate_sig))).astype(jnp.bfloat16)
    up_grad = (hidden_grad * gate_act).astype(jnp.bfloat16)
    term_gate = jnp.dot(gate_grad.T, x_rows, preferred_element_type=jnp.float32)
    term_up = jnp.dot(up_grad.T, x_rows, preferred_element_type=jnp.float32)
    term_down = jnp.dot(hidden.T, q_rows, preferred_element_type=jnp.float32)
    return (term_gate, term_up, term_down)


def reference(tokens, out_grad, expert_ids, route_weight, gate_proj, up_proj, down_proj, fragment):
    most_rows = N_EXPERT * CAP

    def one_pair(pair):
        replica_at = pair // WIN
        expert_at = pair % WIN
        routed = expert_ids[replica_at]
        matches = routed == expert_at
        member = jnp.any(matches, axis=1)
        weight = jnp.sum(jnp.where(matches, route_weight[replica_at], jnp.zeros((), route_weight.dtype)), axis=1)
        count = jnp.sum(member.astype(jnp.int32))
        picked = jnp.nonzero(member, size=most_rows, fill_value=0)[0]
        valid = (jnp.arange(most_rows) < count)[:, None]
        x_rows = jnp.where(valid, tokens[replica_at][picked], jnp.zeros((), tokens.dtype))
        q_rows = jnp.where(valid, weight[picked][:, None] * out_grad[replica_at][picked], 0.0).astype(jnp.bfloat16)
        terms = expert_terms(x_rows, q_rows, gate_proj[expert_at], up_proj[expert_at], down_proj[expert_at])
        return (terms[0], terms[1], terms[2], count)

    results = lax.map(one_pair, jnp.arange(N_REPLICA * WIN))
    frag_width = D // FRAGS
    begin = fragment[0] * frag_width
    columns = jnp.arange(D)
    inside = (columns >= begin) & (columns < begin + frag_width)
    outputs = []
    for stacked in results[:3]:
        grads = stacked.reshape(N_REPLICA, WIN, FF, D)
        synced = jnp.sum(grads, axis=0, keepdims=True) / N_REPLICA
        outputs.append(jnp.where(inside, synced, grads).astype(jnp.bfloat16))
    expert_load = results[3].reshape(N_REPLICA, WIN).astype(jnp.float32) / (WIN * CAP)
    return (outputs[0], outputs[1], outputs[2], expert_load)
```

```python
import functools

import jax
import jax.numpy as jnp
from jax import lax
from jax.experimental import pallas as pl
from jax.experimental.pallas import tpu as pltpu
from jax.sharding import PartitionSpec as P

FRAGS = 4
CAP = 60
SLOTS = 64
F32 = jnp.float32
BF16 = jnp.bfloat16
VMEM = pl.BlockSpec(memory_space=pltpu.VMEM)
SMEM = pl.BlockSpec(memory_space=pltpu.SMEM)
ANY = pl.BlockSpec(memory_space=pl.ANY)


def dot(left, right, left_dim=1, right_dim=0):
    return lax.dot_general(
        left, right, (((left_dim,), (right_dim,)), ((), ())), preferred_element_type=F32
    )


def swap_to_lanes(eye, array):
    return dot(eye, array, 1, 1)


def pack_kernel(experts, tok_ref, grad_ref, ids_ref, weight_ref, *out_refs):
    me = lax.axis_index("expert")
    first = lax.axis_index("tensor") == 0
    tokens, top = ids_ref.shape
    eye = (
        lax.broadcasted_iota(jnp.int32, (top, top), 0)
        == lax.broadcasted_iota(jnp.int32, (top, top), 1)
    ).astype(F32).astype(BF16)
    ids = swap_to_lanes(eye, ids_ref[...].astype(F32).astype(BF16))
    weight = weight_ref[...]
    high = weight.astype(BF16)
    rest = weight - high.astype(F32)
    middle = rest.astype(BF16)
    low = (rest - middle.astype(F32)).astype(BF16)
    weight = (swap_to_lanes(eye, high) + swap_to_lanes(eye, middle)) + swap_to_lanes(eye, low)
    members, weights = [], []
    for step in range(experts):
        expert = lax.rem(me + step, experts).astype(F32)
        match = ids == expert
        members.append(jnp.max(jnp.where(match, 1.0, 0.0), axis=0, keepdims=True))
        weights.append(jnp.sum(jnp.where(match, weight, 0.0), axis=0, keepdims=True))
    member = jnp.concatenate(members, axis=0)
    earlier = (
        lax.broadcasted_iota(jnp.int32, (tokens, tokens), 0)
        < lax.broadcasted_iota(jnp.int32, (tokens, tokens), 1)
    ).astype(F32).astype(BF16)
    position = dot(member.astype(BF16), earlier)
    slot = lax.broadcasted_iota(jnp.int32, (SLOTS, tokens), 0).astype(F32)
    rows = lax.broadcasted_iota(jnp.int32, (SLOTS, 1), 0)
    source = jnp.where(first, tok_ref[...], grad_ref[...])
    for step in range(experts):
        hit = (slot == position[step : step + 1, :]) & (member[step : step + 1, :] > 0.5)
        pick = jnp.where(hit, 1.0, 0.0)
        scale = jnp.sum(pick * weights[step], axis=1, keepdims=True)
        scale = jnp.where(first, 1.0, scale)
        packed = dot(pick.astype(BF16), source) * scale
        count = jnp.sum(members[step], axis=1, keepdims=True)
        packed = jnp.where((rows == CAP) & first, count, packed)
        out_refs[step][...] = packed.astype(BF16)


def pack(experts, tokens, out_grad, ids, weight):
    width = tokens.shape[1]
    return pl.pallas_call(
        functools.partial(pack_kernel, experts),
        out_shape=[jax.ShapeDtypeStruct((SLOTS, width), BF16)] * experts,
        in_specs=[VMEM] * 4,
        out_specs=[VMEM] * experts,
        name="pack",
    )(tokens, out_grad, ids, weight)


def join(mine, theirs, x_rows, q_rows):
    first = lax.axis_index("tensor") == 0
    for step, (here, there) in enumerate(zip(mine, theirs)):
        place = pl.ds(step * SLOTS, SLOTS)
        x_rows[place, :] = jnp.where(first, here[...], there[...])
        q_rows[place, :] = jnp.where(first, there[...], here[...])


def activations(x_rows, q_rows, w_gate, w_up, w_down):
    gate_pre = dot(w_gate[...], x_rows[...], 1, 1)
    up_pre = dot(w_up[...], x_rows[...], 1, 1)
    hidden_grad = dot(w_down[...], q_rows[...], 1, 1)
    gate_sig = jax.nn.sigmoid(gate_pre)
    gate_act = gate_pre * gate_sig
    hidden = (gate_act * up_pre).astype(BF16)
    gate_grad = (hidden_grad * up_pre * gate_sig * (1.0 + gate_pre * (1.0 - gate_sig))).astype(BF16)
    up_grad = (hidden_grad * gate_act).astype(BF16)
    return gate_grad, up_grad, hidden


def own_kernel(experts, frag_ref, *refs):
    mine, theirs = refs[:experts], refs[experts : 2 * experts]
    w_gate, w_up, w_down = refs[2 * experts : 2 * experts + 3]
    outs = refs[2 * experts + 3 : 2 * experts + 6]
    frag_out, load_out, x_rows, q_rows = refs[2 * experts + 6 :]
    join(mine, theirs, x_rows, q_rows)
    total = jnp.zeros((1, 128), F32)
    for step in range(experts):
        total += x_rows[pl.ds(step * SLOTS + CAP, 1), pl.ds(0, 128)].astype(F32)
    load_out[...] = total / (experts * CAP)
    acts = activations(x_rows, q_rows, w_gate, w_up, w_down)
    frag = frag_ref[0]
    cut = frag_out.shape[2]
    for piece, (act, rows, out) in enumerate(zip(acts, (x_rows, x_rows, q_rows), outs)):
        for at in range(FRAGS):
            columns = pl.ds(at * cut, cut)
            grad = dot(act, rows[:, columns])
            out[:, columns] = grad.astype(BF16)

            @pl.when(frag == at)
            def _():
                frag_out[piece] = grad


def own(experts, fragment, mine, theirs, weights):
    units, width = weights[0].shape
    cut = width // FRAGS
    return pl.pallas_call(
        functools.partial(own_kernel, experts),
        out_shape=[jax.ShapeDtypeStruct((units, width), BF16)] * 3
        + [jax.ShapeDtypeStruct((3, units, cut), F32), jax.ShapeDtypeStruct((1, 128), F32)],
        in_specs=[SMEM] + [VMEM] * (2 * experts + 3),
        out_specs=[VMEM] * 5,
        scratch_shapes=[pltpu.VMEM((experts * SLOTS, width), BF16)] * 2,
        name="own",
    )(fragment, *mine, *theirs, *weights)


def other_kernel(experts, frag_ref, *refs):
    mine, theirs = refs[:experts], refs[experts : 2 * experts]
    w_gate, w_up, w_down = refs[2 * experts : 2 * experts + 3]
    frag_in = refs[2 * experts + 3]
    outs = refs[2 * experts + 7 : 2 * experts + 10]
    x_rows, q_rows, cuts, sems = refs[2 * experts + 10 :]
    join(mine, theirs, x_rows, q_rows)
    acts = activations(x_rows, q_rows, w_gate, w_up, w_down)
    cut = frag_in.shape[2]
    columns = pl.ds(pl.multiple_of(frag_ref[0] * cut, cut), cut)
    copies = []
    for piece, (act, rows) in enumerate(zip(acts, (x_rows, x_rows, q_rows))):
        grad = dot(act, rows[:, columns])
        cuts[piece] = ((frag_in[piece] + grad) * 0.5).astype(BF16)
        copies.append(
            pltpu.make_async_copy(cuts.at[piece], outs[piece].at[:, columns], sems.at[piece])
        )
        copies[-1].start()
    for copy in copies:
        copy.wait()


def other(experts, fragment, mine, theirs, weights, frag_grad, grads):
    units, width = weights[0].shape
    cut = width // FRAGS
    at = 1 + 2 * experts + 4
    return pl.pallas_call(
        functools.partial(other_kernel, experts),
        out_shape=[jax.ShapeDtypeStruct((units, width), BF16)] * 3,
        in_specs=[SMEM] + [VMEM] * (2 * experts + 4) + [ANY] * 3,
        out_specs=[ANY] * 3,
        scratch_shapes=[pltpu.VMEM((experts * SLOTS, width), BF16)] * 2
        + [pltpu.VMEM((3, units, cut), BF16), pltpu.SemaphoreType.DMA((3,))],
        input_output_aliases={at: 0, at + 1: 1, at + 2: 2},
        name="other",
    )(fragment, *mine, *theirs, *weights, frag_grad, *grads)


def shift(axis, step):
    size = lax.axis_size(axis)
    return [(index, (index + step) % size) for index in range(size)]


def send(array, axis, step):
    return lax.ppermute(array, axis, shift(axis, step))


def per_device(tokens, out_grad, expert_ids, route_weight, gate_proj, up_proj, down_proj, fragment):
    experts = lax.axis_size("expert")
    replicas = lax.axis_size("replica")
    weights = (gate_proj[0], up_proj[0], down_proj[0])
    packed = pack(experts, tokens[0], out_grad[0], expert_ids[0], route_weight[0])
    mine = [packed[0]] + [send(packed[step], "expert", step) for step in range(1, experts)]
    theirs = [send(rows, "tensor", 1) for rows in mine]
    *grads, frag_grad, load = own(experts, fragment, mine, theirs, weights)
    if replicas == 2:
        far = [send(rows, "replica", 1) for rows in mine]
        far_theirs = [send(rows, "tensor", 1) for rows in far]
        grads = other(experts, fragment, far, far_theirs, weights, frag_grad, grads)
    else:
        synced = lax.psum(frag_grad.astype(BF16), "replica").astype(F32)
        begin = fragment[0] * (weights[0].shape[1] // FRAGS)
        grads = [
            lax.dynamic_update_slice_in_dim(grad, (piece / replicas).astype(BF16), begin, 1)
            for grad, piece in zip(grads, synced)
        ]
    return tuple(grad[None, None] for grad in grads) + (load[:, :1],)


def solution(mesh):
    rows = P(("group", "replica"), "expert", None)
    units = P("expert", "tensor", None)
    grad = P(("group", "replica"), "expert", "tensor", None)
    return jax.shard_map(
        per_device,
        mesh=mesh,
        in_specs=(rows, rows, rows, rows, units, units, units, P("group")),
        out_specs=(grad, grad, grad, P(("group", "replica"), "expert")),
        check_vma=False,
    )
```

```python
import functools

import jax
import jax.numpy as jnp
from jax import lax
from jax.experimental import pallas as pl
from jax.experimental.pallas import tpu as pltpu
from jax.sharding import PartitionSpec as P

FRAGS = 4
CAP = 60
SLOTS = 64
F32 = jnp.float32
BF16 = jnp.bfloat16
VMEM = pl.BlockSpec(memory_space=pltpu.VMEM)
SMEM = pl.BlockSpec(memory_space=pltpu.SMEM)
ANY = pl.BlockSpec(memory_space=pl.ANY)
HBM = pl.BlockSpec(memory_space=pltpu.HBM)


def dot(left, right, left_dim=1, right_dim=0):
    return lax.dot_general(
        left, right, (((left_dim,), (right_dim,)), ((), ())), preferred_element_type=F32
    )


def peer(index, step, size):
    return index ^ step if size & (size - 1) == 0 else (index + step) % size


def pack_kernel(experts, parts, tok_hbm, grad_hbm, ids_hbm, weight_hbm, *refs):
    out_refs, (source_ref, ids_ref, weight_ref, sems) = refs[:experts], refs[experts:]
    me = lax.axis_index("expert")
    first = lax.axis_index("tensor") == 0
    tokens = ids_ref.shape[1]
    ids_copy = pltpu.make_async_copy(ids_hbm, ids_ref, sems.at[parts])
    weight_copy = pltpu.make_async_copy(weight_hbm, weight_ref, sems.at[parts + 1])
    ids_copy.start()
    weight_copy.start()
    step_rows = tokens // parts

    def fetch(hbm):
        return [
            pltpu.make_async_copy(
                hbm.at[pl.ds(part * step_rows, step_rows), :],
                source_ref.at[pl.ds(part * step_rows, step_rows), :],
                sems.at[part],
            )
            for part in range(parts)
        ]

    @pl.when(first)
    def _():
        for copy in fetch(tok_hbm):
            copy.start()

    @pl.when(jnp.logical_not(first))
    def _():
        for copy in fetch(grad_hbm):
            copy.start()

    ids_copy.wait()
    weight_copy.wait()
    ids = ids_ref[...]
    weight = weight_ref[...]
    members, weights = [], []
    for step in range(experts):
        match = ids == peer(me, step, experts)
        members.append(jnp.max(jnp.where(match, 1.0, 0.0), axis=0, keepdims=True))
        weights.append(jnp.sum(jnp.where(match, weight, 0.0), axis=0, keepdims=True))
    member = jnp.concatenate(members, axis=0)
    earlier = (
        lax.broadcasted_iota(jnp.int32, (tokens, tokens), 0)
        < lax.broadcasted_iota(jnp.int32, (tokens, tokens), 1)
    ).astype(F32).astype(BF16)
    position = dot(member.astype(BF16), earlier)
    slot = lax.broadcasted_iota(jnp.int32, (SLOTS, tokens), 0).astype(F32)
    rows = lax.broadcasted_iota(jnp.int32, (SLOTS, 1), 0)

    @pl.when(first)
    def _():
        for copy in fetch(tok_hbm):
            copy.wait()

    @pl.when(jnp.logical_not(first))
    def _():
        for copy in fetch(grad_hbm):
            copy.wait()

    source = source_ref[...]
    for step in range(experts):
        hit = (slot == position[step : step + 1, :]) & (member[step : step + 1, :] > 0.5)
        pick = jnp.where(hit, 1.0, 0.0)
        scale = jnp.sum(pick * weights[step], axis=1, keepdims=True)
        scale = jnp.where(first, 1.0, scale)
        packed = dot(pick.astype(BF16), source) * scale
        count = jnp.sum(members[step], axis=1, keepdims=True)
        packed = jnp.where((rows == CAP) & first, count, packed)
        out_refs[step][...] = packed.astype(BF16)


def in_hbm(array):
    return pltpu.with_memory_space_constraint(array, pltpu.HBM)


def load_kernel(count, *refs):
    sources, targets, sems = refs[:count], refs[count + 1 : 2 * count + 1], refs[-1]
    copies = [
        pltpu.make_async_copy(source, target, sems.at[index])
        for index, (source, target) in enumerate(zip(sources, targets))
    ]
    for copy in copies:
        copy.start()
    for copy in copies:
        copy.wait()


def load(arrays, after):
    count = len(arrays)
    return pl.pallas_call(
        functools.partial(load_kernel, count),
        out_shape=[pltpu.VMEM(array.shape, array.dtype) for array in arrays],
        in_specs=[HBM] * count + [ANY],
        out_specs=[VMEM] * count,
        scratch_shapes=[pltpu.SemaphoreType.DMA((count,))],
        compiler_params=pltpu.CompilerParams(vmem_limit_bytes=8 << 20),
        name="load",
    )(*[in_hbm(array) for array in arrays], after)


def pack(experts, tokens, out_grad, ids, weight):
    count, width = tokens.shape
    parts = 5 if count % 80 == 0 else 1
    inputs = [in_hbm(array) for array in (tokens, out_grad, ids.T, weight.T)]
    return pl.pallas_call(
        functools.partial(pack_kernel, experts, parts),
        out_shape=[pltpu.VMEM((SLOTS, width), BF16)] * experts,
        in_specs=[HBM] * 4,
        out_specs=[VMEM] * experts,
        scratch_shapes=[
            pltpu.VMEM((count, width), BF16),
            pltpu.VMEM(ids.shape[::-1], jnp.int32),
            pltpu.VMEM(ids.shape[::-1], F32),
            pltpu.SemaphoreType.DMA((parts + 2,)),
        ],
        name="pack",
        compiler_params=pltpu.CompilerParams(vmem_limit_bytes=16 << 20),
    )(*inputs)


def join(mine, theirs, x_rows, q_rows):
    first = lax.axis_index("tensor") == 0
    for step, (here, there) in enumerate(zip(mine, theirs)):
        place = pl.ds(step * SLOTS, SLOTS)
        x_rows[place, :] = jnp.where(first, here[...], there[...])
        q_rows[place, :] = jnp.where(first, there[...], here[...])


def activations(x_rows, q_rows, w_gate, w_up, w_down):
    gate_pre = dot(w_gate[...], x_rows[...], 1, 1)
    up_pre = dot(w_up[...], x_rows[...], 1, 1)
    hidden_grad = dot(w_down[...], q_rows[...], 1, 1)
    gate_sig = jax.nn.sigmoid(gate_pre)
    gate_act = gate_pre * gate_sig
    hidden = (gate_act * up_pre).astype(BF16)
    gate_grad = (hidden_grad * up_pre * gate_sig * (1.0 + gate_pre * (1.0 - gate_sig))).astype(BF16)
    up_grad = (hidden_grad * gate_act).astype(BF16)
    return gate_grad, up_grad, hidden


def own_kernel(experts, frag_ref, *refs):
    mine, theirs = refs[:experts], refs[experts : 2 * experts]
    w_gate, w_up, w_down = refs[2 * experts : 2 * experts + 3]
    outs = refs[2 * experts + 3 : 2 * experts + 6]
    frag_out, load_out, x_rows, q_rows, stage, sems = refs[2 * experts + 6 :]
    join(mine, theirs, x_rows, q_rows)
    total = jnp.zeros((1, 128), F32)
    for step in range(experts):
        total += x_rows[pl.ds(step * SLOTS + CAP, 1), pl.ds(0, 128)].astype(F32)
    load_out[...] = total / (experts * CAP)
    acts = activations(x_rows, q_rows, w_gate, w_up, w_down)
    cut = frag_out.shape[2]
    frag_columns = pl.ds(pl.multiple_of(frag_ref[0] * cut, cut), cut)
    copies = []
    for piece, (act, rows, out) in enumerate(zip(acts, (x_rows, x_rows, q_rows), outs)):
        for at in range(FRAGS):
            columns = pl.ds(at * cut, cut)
            stage[piece, :, columns] = dot(act, rows[:, columns]).astype(BF16)
        copies.append(pltpu.make_async_copy(stage.at[piece], out, sems.at[piece]))
        copies[-1].start()
        frag_out[piece] = dot(act, rows[:, frag_columns])
    for copy in copies:
        copy.wait()


def own(experts, fragment, mine, theirs, weights):
    units, width = weights[0].shape
    cut = width // FRAGS
    return pl.pallas_call(
        functools.partial(own_kernel, experts),
        out_shape=[jax.ShapeDtypeStruct((units, width), BF16)] * 3
        + [pltpu.VMEM((3, units, cut), F32), jax.ShapeDtypeStruct((1, 128), F32)],
        in_specs=[SMEM] + [VMEM] * (2 * experts + 3),
        out_specs=[HBM] * 3 + [VMEM] * 2,
        scratch_shapes=[pltpu.VMEM((experts * SLOTS, width), BF16)] * 2
        + [pltpu.VMEM((3, units, width), BF16), pltpu.SemaphoreType.DMA((3,))],
        name="own",
        compiler_params=pltpu.CompilerParams(vmem_limit_bytes=32 << 20),
        cost_estimate=pl.CostEstimate(
            flops=12 * units * width * experts * SLOTS, bytes_accessed=12 * units * width, transcendentals=0
        ),
    )(fragment, *mine, *theirs, *weights)


def other_kernel(experts, frag_ref, *refs):
    mine, theirs = refs[:experts], refs[experts : 2 * experts]
    w_gate, w_up, w_down = refs[2 * experts : 2 * experts + 3]
    frag_in = refs[2 * experts + 3]
    outs = refs[2 * experts + 7 : 2 * experts + 10]
    x_rows, q_rows, cuts, sems = refs[2 * experts + 10 :]
    join(mine, theirs, x_rows, q_rows)
    acts = activations(x_rows, q_rows, w_gate, w_up, w_down)
    cut = frag_in.shape[2]
    columns = pl.ds(pl.multiple_of(frag_ref[0] * cut, cut), cut)
    copies = []
    for piece, (act, rows) in enumerate(zip(acts, (x_rows, x_rows, q_rows))):
        grad = dot(act, rows[:, columns])
        cuts[piece] = ((frag_in[piece] + grad) * 0.5).astype(BF16)
        copies.append(
            pltpu.make_async_copy(cuts.at[piece], outs[piece].at[:, columns], sems.at[piece])
        )
        copies[-1].start()
    for copy in copies:
        copy.wait()


def other(experts, fragment, mine, theirs, weights, frag_grad, grads):
    units, width = weights[0].shape
    cut = width // FRAGS
    at = 1 + 2 * experts + 4
    return pl.pallas_call(
        functools.partial(other_kernel, experts),
        out_shape=[jax.ShapeDtypeStruct((units, width), BF16)] * 3,
        in_specs=[SMEM] + [VMEM] * (2 * experts + 4) + [ANY] * 3,
        out_specs=[ANY] * 3,
        scratch_shapes=[pltpu.VMEM((experts * SLOTS, width), BF16)] * 2
        + [pltpu.VMEM((3, units, cut), BF16), pltpu.SemaphoreType.DMA((3,))],
        input_output_aliases={at: 0, at + 1: 1, at + 2: 2},
        name="other",
        compiler_params=pltpu.CompilerParams(vmem_limit_bytes=32 << 20),
        cost_estimate=pl.CostEstimate(
            flops=8 * units * width * experts * SLOTS, bytes_accessed=8 * units * width, transcendentals=0
        ),
    )(fragment, *mine, *theirs, *weights, frag_grad, *grads)


def send(array, axis, step):
    size = lax.axis_size(axis)
    return lax.ppermute(array, axis, [(index, peer(index, step, size)) for index in range(size)])


def tie(*arrays):
    return lax.optimization_barrier(arrays)


def two_replicas(fragment, packed, weights):
    r0 = packed[0]
    r2 = send(packed[2], "expert", 2)
    x0 = send(r0, "replica", 1)
    r1 = send(packed[1], "expert", 1)
    r3 = send(packed[3], "expert", 3)
    x1 = send(packed[1], ("expert", "replica"), 3)
    weights = load(weights, r0)
    r2, x0, x1, *weights = tie(r2, x0, x1, *weights)
    c0 = send(r0, "tensor", 1)
    c1 = send(r1, "tensor", 1)
    f0 = send(x0, "tensor", 1)
    c2 = send(r2, "tensor", 1)
    x2 = send(r2, "replica", 1)
    r3, c0, c1, f0, x1 = tie(r3, c0, c1, f0, x1)
    c3 = send(r3, "tensor", 1)
    x3 = send(r3, "replica", 1)
    c3, x2 = tie(c3, x2)
    mine = [r0, r1, r2, r3]
    theirs = [c0, c1, c2, c3]
    *grads, frag_grad, filled = own(4, fragment, mine, theirs, weights)
    x1, x2, x3, filled = tie(x1, x2, x3, filled)
    f1 = send(x1, "tensor", 1)
    f2 = send(x2, "tensor", 1)
    f3 = send(x3, "tensor", 1)
    far = [x0, x1, x2, x3]
    far_theirs = [f0, f1, f2, f3]
    grads = other(4, fragment, far, far_theirs, weights, frag_grad, grads)
    return grads, filled


def any_replicas(experts, replicas, fragment, packed, weights):
    mine = [packed[0]] + [send(packed[step], "expert", step) for step in range(1, experts)]
    theirs = [send(rows, "tensor", 1) for rows in mine]
    *grads, frag_grad, filled = own(experts, fragment, mine, theirs, weights)
    synced = lax.psum(frag_grad.astype(BF16), "replica").astype(F32)
    begin = fragment[0] * (weights[0].shape[1] // FRAGS)
    grads = [
        lax.dynamic_update_slice_in_dim(grad, (piece / replicas).astype(BF16), begin, 1)
        for grad, piece in zip(grads, synced)
    ]
    return grads, filled


def per_device(tokens, out_grad, expert_ids, route_weight, gate_proj, up_proj, down_proj, fragment):
    experts = lax.axis_size("expert")
    replicas = lax.axis_size("replica")
    weights = (gate_proj[0], up_proj[0], down_proj[0])
    packed = pack(experts, tokens[0], out_grad[0], expert_ids[0], route_weight[0])
    if replicas == 2 and experts == 4:
        grads, filled = two_replicas(fragment, packed, weights)
    else:
        grads, filled = any_replicas(experts, replicas, fragment, packed, weights)
    return tuple(grad[None, None] for grad in grads) + (filled[:, :1],)


def solution(mesh):
    rows = P(("group", "replica"), "expert", None)
    units = P("expert", "tensor", None)
    grad = P(("group", "replica"), "expert", "tensor", None)
    return jax.shard_map(
        per_device,
        mesh=mesh,
        in_specs=(rows, rows, rows, rows, units, units, units, P("group")),
        out_specs=(grad, grad, grad, P(("group", "replica"), "expert")),
        check_vma=False,
    )
```

```python
import functools

import jax
import jax.numpy as jnp
from jax import lax
from jax.experimental import pallas as pl
from jax.experimental.pallas import tpu as pltpu
from jax.sharding import PartitionSpec as P

FRAGS = 4
CAP = 60
SLOTS = 64
F32 = jnp.float32
BF16 = jnp.bfloat16
VMEM = pl.BlockSpec(memory_space=pltpu.VMEM)
SMEM = pl.BlockSpec(memory_space=pltpu.SMEM)
ANY = pl.BlockSpec(memory_space=pl.ANY)
HBM = pl.BlockSpec(memory_space=pltpu.HBM)


def dot(left, right, left_dim=1, right_dim=0):
    return lax.dot_general(
        left, right, (((left_dim,), (right_dim,)), ((), ())), preferred_element_type=F32
    )


def peer(index, step, size):
    return index ^ step if size & (size - 1) == 0 else (index + step) % size


def pack_kernel(experts, parts, tok_hbm, grad_hbm, ids_hbm, weight_hbm, *refs):
    *out_refs, source_ref, ids_ref, weight_ref, sems = refs
    me = lax.axis_index("expert")
    first = lax.axis_index("tensor") == 0
    tokens = ids_ref.shape[1]
    ids_copy = pltpu.make_async_copy(ids_hbm, ids_ref, sems.at[parts])
    weight_copy = pltpu.make_async_copy(weight_hbm, weight_ref, sems.at[parts + 1])
    ids_copy.start()
    weight_copy.start()
    step_rows = tokens // parts

    def fetch(hbm):
        return [
            pltpu.make_async_copy(
                hbm.at[pl.ds(part * step_rows, step_rows), :],
                source_ref.at[pl.ds(part * step_rows, step_rows), :],
                sems.at[part],
            )
            for part in range(parts)
        ]

    @pl.when(first)
    def _():
        for copy in fetch(tok_hbm):
            copy.start()

    @pl.when(jnp.logical_not(first))
    def _():
        for copy in fetch(grad_hbm):
            copy.start()

    ids_copy.wait()
    weight_copy.wait()
    ids = ids_ref[...]
    weight = weight_ref[...]
    members, weights = [], []
    for step in range(experts):
        match = ids == peer(me, step, experts)
        members.append(jnp.max(jnp.where(match, 1.0, 0.0), axis=0, keepdims=True))
        weights.append(jnp.sum(jnp.where(match, weight, 0.0), axis=0, keepdims=True))
    member = jnp.concatenate(members, axis=0)
    earlier = (
        lax.broadcasted_iota(jnp.int32, (tokens, tokens), 0)
        < lax.broadcasted_iota(jnp.int32, (tokens, tokens), 1)
    ).astype(F32).astype(BF16)
    position = dot(member.astype(BF16), earlier)
    slot = lax.broadcasted_iota(jnp.int32, (SLOTS, tokens), 0).astype(F32)
    rows = lax.broadcasted_iota(jnp.int32, (SLOTS, 1), 0)

    @pl.when(first)
    def _():
        for copy in fetch(tok_hbm):
            copy.wait()

    @pl.when(jnp.logical_not(first))
    def _():
        for copy in fetch(grad_hbm):
            copy.wait()

    source = source_ref[...]
    for step in range(experts):
        hit = (slot == position[step : step + 1, :]) & (member[step : step + 1, :] > 0.5)
        pick = jnp.where(hit, 1.0, 0.0)
        scale = jnp.sum(pick * weights[step], axis=1, keepdims=True)
        scale = jnp.where(first, 1.0, scale)
        packed = dot(pick.astype(BF16), source) * scale
        count = jnp.sum(members[step], axis=1, keepdims=True)
        packed = jnp.where((rows == CAP) & first, count, packed)
        packed = packed.astype(BF16)
        for out in out_refs[step:] if step == experts - 1 else out_refs[step : step + 1]:
            out[...] = packed[: out.shape[0], :]
            packed = packed[out.shape[0] :, :]


def in_hbm(array):
    return pltpu.with_memory_space_constraint(array, pltpu.HBM)


def load_kernel(count, *refs):
    sources, targets, sems = refs[:count], refs[count + 2 : 2 * count + 2], refs[-1]
    copies = [
        pltpu.make_async_copy(source, target, sems.at[index])
        for index, (source, target) in enumerate(zip(sources, targets))
    ]
    for copy in copies:
        copy.start()
    for copy in copies:
        copy.wait()


def load(arrays, fragment, after):
    count = len(arrays)
    return pl.pallas_call(
        functools.partial(load_kernel, count),
        out_shape=[pltpu.VMEM(array.shape, array.dtype) for array in arrays],
        in_specs=[HBM] * count + [SMEM, ANY],
        out_specs=[VMEM] * count,
        scratch_shapes=[pltpu.SemaphoreType.DMA((count,))],
        compiler_params=pltpu.CompilerParams(vmem_limit_bytes=8 << 20),
        name="load",
    )(*[in_hbm(array) for array in arrays], fragment, after)


def stack_kernel(*refs):
    *parts, whole = refs
    at = 0
    for part in parts:
        whole[pl.ds(at, part.shape[0]), :] = part[...]
        at += part.shape[0]


def stack(parts):
    rows = sum(part.shape[0] for part in parts)
    return pl.pallas_call(
        stack_kernel,
        out_shape=pltpu.VMEM((rows, parts[0].shape[1]), parts[0].dtype),
        in_specs=[VMEM] * len(parts),
        out_specs=VMEM,
        compiler_params=pltpu.CompilerParams(vmem_limit_bytes=8 << 20),
        name="stack",
    )(*parts)


def pack(experts, rows, tokens, out_grad, ids, weight):
    width = tokens.shape[1]
    parts = 5 if tokens.shape[0] % 80 == 0 else 1
    inputs = [in_hbm(array) for array in (tokens, out_grad, ids.T, weight.T)]
    return pl.pallas_call(
        functools.partial(pack_kernel, experts, parts),
        out_shape=[pltpu.VMEM((count, width), BF16) for count in rows],
        in_specs=[HBM] * 4,
        out_specs=[VMEM] * len(rows),
        scratch_shapes=[
            pltpu.VMEM((tokens.shape[0], width), BF16),
            pltpu.VMEM(ids.shape[::-1], jnp.int32),
            pltpu.VMEM(ids.shape[::-1], F32),
            pltpu.SemaphoreType.DMA((parts + 2,)),
        ],
        name="pack",
        compiler_params=pltpu.CompilerParams(vmem_limit_bytes=16 << 20),
    )(*inputs)


def join(mine, theirs, x_rows, q_rows):
    first = lax.axis_index("tensor") == 0
    at = 0
    for here, there in zip(mine, theirs):
        place = pl.ds(at, here.shape[0])
        x_rows[place, :] = jnp.where(first, here[...], there[...])
        q_rows[place, :] = jnp.where(first, there[...], here[...])
        at += here.shape[0]


def activations(x_rows, q_rows, w_gate, w_up, w_down):
    gate_pre = dot(w_gate[...], x_rows[...], 1, 1)
    up_pre = dot(w_up[...], x_rows[...], 1, 1)
    hidden_grad = dot(w_down[...], q_rows[...], 1, 1)
    gate_sig = jax.nn.sigmoid(gate_pre)
    gate_act = gate_pre * gate_sig
    hidden = (gate_act * up_pre).astype(BF16)
    gate_grad = (hidden_grad * up_pre * gate_sig * (1.0 + gate_pre * (1.0 - gate_sig))).astype(BF16)
    up_grad = (hidden_grad * gate_act).astype(BF16)
    return gate_grad, up_grad, hidden


def own_kernel(experts, pieces, frag_ref, *refs):
    mine, theirs = refs[:pieces], refs[pieces : 2 * pieces]
    w_gate, w_up, w_down = refs[2 * pieces : 2 * pieces + 3]
    outs = refs[2 * pieces + 3 : 2 * pieces + 6]
    frag_out, load_out, x_rows, q_rows, stage, sems = refs[2 * pieces + 6 :]
    join(mine, theirs, x_rows, q_rows)
    total = jnp.zeros((1, 128), F32)
    for step in range(experts):
        total += x_rows[pl.ds(step * SLOTS + CAP, 1), pl.ds(0, 128)].astype(F32)
    load_out[...] = total / (experts * CAP)
    acts = activations(x_rows, q_rows, w_gate, w_up, w_down)
    cut = frag_out.shape[2]
    frag_columns = pl.ds(pl.multiple_of(frag_ref[0] * cut, cut), cut)
    copies = []
    for piece, (act, rows, out) in enumerate(zip(acts, (x_rows, x_rows, q_rows), outs)):
        for at in range(FRAGS):
            columns = pl.ds(at * cut, cut)
            stage[piece, :, columns] = dot(act, rows[:, columns]).astype(BF16)
        copies.append(pltpu.make_async_copy(stage.at[piece], out, sems.at[piece]))
        copies[-1].start()
    for piece, (act, rows) in enumerate(zip(acts, (x_rows, x_rows, q_rows))):
        frag_out[piece] = dot(act, rows[:, frag_columns])
    for copy in copies:
        copy.wait()


def own(experts, fragment, mine, theirs, weights):
    units, width = weights[0].shape
    cut = width // FRAGS
    pieces = len(mine)
    return pl.pallas_call(
        functools.partial(own_kernel, experts, pieces),
        out_shape=[jax.ShapeDtypeStruct((units, width), BF16)] * 3
        + [pltpu.VMEM((3, units, cut), F32), jax.ShapeDtypeStruct((1, 128), F32)],
        in_specs=[SMEM] + [VMEM] * (2 * pieces + 3),
        out_specs=[HBM] * 3 + [VMEM] * 2,
        scratch_shapes=[pltpu.VMEM((experts * SLOTS, width), BF16)] * 2
        + [pltpu.VMEM((3, units, width), BF16), pltpu.SemaphoreType.DMA((3,))],
        name="own",
        compiler_params=pltpu.CompilerParams(vmem_limit_bytes=32 << 20),
        cost_estimate=pl.CostEstimate(
            flops=12 * units * width * experts * SLOTS, bytes_accessed=12 * units * width, transcendentals=0
        ),
    )(fragment, *mine, *theirs, *weights)


def other_kernel(pieces, frag_ref, *refs):
    mine, theirs = refs[:pieces], refs[pieces : 2 * pieces]
    w_gate, w_up, w_down = refs[2 * pieces : 2 * pieces + 3]
    frag_in = refs[2 * pieces + 3]
    outs = refs[2 * pieces + 7 : 2 * pieces + 10]
    x_rows, q_rows, cuts, sems = refs[2 * pieces + 10 :]
    join(mine, theirs, x_rows, q_rows)
    acts = activations(x_rows, q_rows, w_gate, w_up, w_down)
    cut = frag_in.shape[2]
    columns = pl.ds(pl.multiple_of(frag_ref[0] * cut, cut), cut)
    copies = []
    for piece, (act, rows) in enumerate(zip(acts, (x_rows, x_rows, q_rows))):
        grad = dot(act, rows[:, columns])
        cuts[piece] = ((frag_in[piece] + grad) * 0.5).astype(BF16)
        copies.append(
            pltpu.make_async_copy(cuts.at[piece], outs[piece].at[:, columns], sems.at[piece])
        )
        copies[-1].start()
    for copy in copies:
        copy.wait()


def other(fragment, mine, theirs, weights, frag_grad, grads):
    units, width = weights[0].shape
    cut = width // FRAGS
    pieces = len(mine)
    rows = sum(part.shape[0] for part in mine)
    at = 1 + 2 * pieces + 4
    return pl.pallas_call(
        functools.partial(other_kernel, pieces),
        out_shape=[jax.ShapeDtypeStruct((units, width), BF16)] * 3,
        in_specs=[SMEM] + [VMEM] * (2 * pieces + 4) + [ANY] * 3,
        out_specs=[ANY] * 3,
        scratch_shapes=[pltpu.VMEM((rows, width), BF16)] * 2
        + [pltpu.VMEM((3, units, cut), BF16), pltpu.SemaphoreType.DMA((3,))],
        input_output_aliases={at: 0, at + 1: 1, at + 2: 2},
        name="other",
        compiler_params=pltpu.CompilerParams(vmem_limit_bytes=32 << 20),
        cost_estimate=pl.CostEstimate(
            flops=8 * units * width * rows, bytes_accessed=8 * units * width, transcendentals=0
        ),
    )(fragment, *mine, *theirs, *weights, frag_grad, *grads)


def send(array, axis, step):
    size = lax.axis_size(axis)
    return lax.ppermute(array, axis, [(index, peer(index, step, size)) for index in range(size)])


def tie(*arrays):
    return lax.optimization_barrier(arrays)


def two_replicas(fragment, packed, weights):
    r0 = packed[0]
    r3 = send(packed[3], "expert", 3)
    x0 = send(r0, "replica", 1)
    r1 = send(packed[1], "expert", 1)
    x1 = send(packed[1], ("expert", "replica"), 3)
    r2 = send(packed[2], "expert", 2)
    weights = load(weights, fragment, r0)
    r3, x0, *weights = tie(r3, x0, *weights)
    x3 = send(r3, "replica", 1)
    r2, x3, r1, x1 = tie(r2, x3, r1, x1)
    x2 = send(r2, "replica", 1)
    near = stack([r0, r1, r3, r2])
    c0 = send(near, "tensor", 1)
    far = stack([x0, x1, x3])
    f0 = send(far, "tensor", 1)
    mine, theirs = [near], [c0]
    *grads, frag_grad, filled = own(4, fragment, mine, theirs, weights)
    x2, filled = tie(x2, filled)
    f3 = send(x2, "tensor", 1)
    grads = other(fragment, [far, x2], [f0, f3], weights, frag_grad, grads)
    return grads, filled


def any_replicas(experts, replicas, fragment, packed, weights):
    mine = [packed[0]] + [send(packed[step], "expert", step) for step in range(1, experts)]
    theirs = [send(rows, "tensor", 1) for rows in mine]
    *grads, frag_grad, filled = own(experts, fragment, mine, theirs, weights)
    synced = lax.psum(frag_grad.astype(BF16), "replica").astype(F32)
    begin = fragment[0] * (weights[0].shape[1] // FRAGS)
    grads = [
        lax.dynamic_update_slice_in_dim(grad, (piece / replicas).astype(BF16), begin, 1)
        for grad, piece in zip(grads, synced)
    ]
    return grads, filled


def per_device(tokens, out_grad, expert_ids, route_weight, gate_proj, up_proj, down_proj, fragment):
    experts = lax.axis_size("expert")
    replicas = lax.axis_size("replica")
    weights = (gate_proj[0], up_proj[0], down_proj[0])
    parts = [SLOTS] * experts
    packed = pack(experts, parts, tokens[0], out_grad[0], expert_ids[0], route_weight[0])
    if replicas == 2 and experts == 4:
        grads, filled = two_replicas(fragment, packed, weights)
    else:
        grads, filled = any_replicas(experts, replicas, fragment, packed, weights)
    return tuple(grad[None, None] for grad in grads) + (filled[:, :1],)


def solution(mesh):
    rows = P(("group", "replica"), "expert", None)
    units = P("expert", "tensor", None)
    grad = P(("group", "replica"), "expert", "tensor", None)
    return jax.shard_map(
        per_device,
        mesh=mesh,
        in_specs=(rows, rows, rows, rows, units, units, units, P("group")),
        out_specs=(grad, grad, grad, P(("group", "replica"), "expert")),
        check_vma=False,
    )
```

```python
import functools

import jax
import jax.numpy as jnp
from jax import lax
from jax.experimental import pallas as pl
from jax.experimental.pallas import tpu as pltpu
from jax.sharding import PartitionSpec as P

FRAGS = 4
CAP = 60
SLOTS = 64
BLOCKS = 4
MAIN = CAP // 16 * 16
REST = CAP - MAIN
EMPTY = 64.0
F32 = jnp.float32
BF16 = jnp.bfloat16
VMEM = pl.BlockSpec(memory_space=pltpu.VMEM)
SMEM = pl.BlockSpec(memory_space=pltpu.SMEM)
ANY = pl.BlockSpec(memory_space=pl.ANY)
HBM = pl.BlockSpec(memory_space=pltpu.HBM)


def dot(left, right, left_dim=1, right_dim=0):
    return lax.dot_general(
        left, right, (((left_dim,), (right_dim,)), ((), ())), preferred_element_type=F32
    )


def peer(index, step, size):
    return index ^ step if size & (size - 1) == 0 else (index + step) % size


def pack_kernel(experts, tok_hbm, grad_hbm, ids_hbm, weight_hbm, *refs):
    *out_refs, source_ref, ids_ref, weight_ref, sems = refs
    me = lax.axis_index("expert")
    first = lax.axis_index("tensor") == 0
    tokens = ids_ref.shape[1]
    ids_copy = pltpu.make_async_copy(ids_hbm, ids_ref, sems.at[0])
    weight_copy = pltpu.make_async_copy(weight_hbm, weight_ref, sems.at[1])
    ids_copy.start()
    weight_copy.start()
    cut = source_ref.shape[1] // BLOCKS
    tok_copy = pltpu.make_async_copy(tok_hbm, source_ref, sems.at[2])
    grad_copy = pltpu.make_async_copy(grad_hbm, source_ref, sems.at[2])

    @pl.when(first)
    def _():
        tok_copy.start()

    @pl.when(jnp.logical_not(first))
    def _():
        grad_copy.start()

    ids_copy.wait()
    weight_copy.wait()
    ids = ids_ref[...]
    weight = weight_ref[...]
    members, weights = [], []
    for step in range(experts):
        match = ids == peer(me, step, experts)
        members.append(jnp.max(jnp.where(match, 1.0, 0.0), axis=0, keepdims=True))
        weights.append(jnp.sum(jnp.where(match, weight, 0.0), axis=0, keepdims=True))
    member = jnp.concatenate(members, axis=0)
    earlier = (
        lax.broadcasted_iota(jnp.int32, (tokens, tokens), 0)
        < lax.broadcasted_iota(jnp.int32, (tokens, tokens), 1)
    ).astype(F32).astype(BF16)
    position = dot(member.astype(BF16), earlier)
    slot = lax.broadcasted_iota(jnp.int32, (SLOTS, tokens), 0).astype(F32)
    rows = lax.broadcasted_iota(jnp.int32, (SLOTS, 1), 0).astype(F32)
    picks, scales, fills = [], [], []
    for step in range(experts):
        hit = (slot == position[step : step + 1, :]) & (member[step : step + 1, :] > 0.5)
        pick = jnp.where(hit, 1.0, 0.0)
        scale = jnp.sum(pick * weights[step], axis=1, keepdims=True)
        scales.append(jnp.where(first, 1.0, scale))
        count = jnp.sum(members[step], axis=1, keepdims=True)
        fills.append(jnp.where((rows >= count) & first, EMPTY, 0.0))
        picks.append(pick.astype(BF16))
    picks = jnp.concatenate(picks, axis=0)
    scales = jnp.concatenate(scales, axis=0)
    fills = jnp.concatenate(fills, axis=0)
    places = rest_places((BLOCKS * REST, BLOCKS * 16), 0, 1)
    tok_copy.wait()
    packed = (dot(picks, source_ref[...]) * scales + fills).astype(BF16)
    rests = []
    for block in range(BLOCKS):
        for step in range(experts):
            tile = packed[step * SLOTS : (step + 1) * SLOTS, block * cut : (block + 1) * cut]
            out_refs[step][pl.ds(block * MAIN, MAIN), :] = tile[:MAIN]
            rests.append(tile[MAIN:])
    for step in range(experts):
        rest = dot(places, jnp.concatenate(rests[step::experts], axis=0))
        out_refs[step][pl.ds(BLOCKS * MAIN, BLOCKS * REST), :] = rest.astype(BF16)


def rest_places(shape, wire, block):
    left = lax.broadcasted_iota(jnp.int32, shape, wire)
    right = lax.broadcasted_iota(jnp.int32, shape, block)
    hit = (lax.rem(right, 16) < REST) & (left == right // 16 * REST + lax.rem(right, 16))
    return hit.astype(F32).astype(BF16)


def in_hbm(array):
    return pltpu.with_memory_space_constraint(array, pltpu.HBM)


def load_kernel(count, *refs):
    sources, targets, sems = refs[:count], refs[count + 2 : 2 * count + 2], refs[-1]
    copies = [
        pltpu.make_async_copy(source, target, sems.at[index])
        for index, (source, target) in enumerate(zip(sources, targets))
    ]
    for copy in copies:
        copy.start()
    for copy in copies:
        copy.wait()


def load(arrays, fragment, after):
    count = len(arrays)
    return pl.pallas_call(
        functools.partial(load_kernel, count),
        out_shape=[pltpu.VMEM(array.shape, array.dtype) for array in arrays],
        in_specs=[HBM] * count + [SMEM, ANY],
        out_specs=[VMEM] * count,
        scratch_shapes=[pltpu.SemaphoreType.DMA((count,))],
        compiler_params=pltpu.CompilerParams(vmem_limit_bytes=8 << 20),
        name="load",
    )(*[in_hbm(array) for array in arrays], fragment, after)


def stack_kernel(*refs):
    *parts, whole = refs
    at = 0
    for part in parts:
        whole[pl.ds(at, part.shape[0]), :] = part[...]
        at += part.shape[0]


def stack(parts):
    rows = sum(part.shape[0] for part in parts)
    return pl.pallas_call(
        stack_kernel,
        out_shape=pltpu.VMEM((rows, parts[0].shape[1]), parts[0].dtype),
        in_specs=[VMEM] * len(parts),
        out_specs=VMEM,
        compiler_params=pltpu.CompilerParams(vmem_limit_bytes=8 << 20),
        name="stack",
    )(*parts)


def pack(experts, tokens, out_grad, ids, weight):
    width = tokens.shape[1]
    inputs = [in_hbm(array) for array in (tokens, out_grad, ids.T, weight.T)]
    return pl.pallas_call(
        functools.partial(pack_kernel, experts),
        out_shape=[pltpu.VMEM((BLOCKS * CAP, width // BLOCKS), BF16)] * experts,
        in_specs=[HBM] * 4,
        out_specs=[VMEM] * experts,
        scratch_shapes=[
            pltpu.VMEM((tokens.shape[0], width), BF16),
            pltpu.VMEM(ids.shape[::-1], jnp.int32),
            pltpu.VMEM(ids.shape[::-1], F32),
            pltpu.SemaphoreType.DMA((3,)),
        ],
        name="pack",
        compiler_params=pltpu.CompilerParams(vmem_limit_bytes=16 << 20),
    )(*inputs)


def join(mine, theirs, x_rows, q_rows):
    first = lax.axis_index("tensor") == 0
    width = x_rows.shape[1]
    cut = width // BLOCKS
    places = rest_places((BLOCKS * 16, BLOCKS * REST), 1, 0)
    chunk = 0
    for here, there in zip(mine, theirs):
        for at in range(0, here.shape[0], BLOCKS * CAP):
            for block in range(BLOCKS):
                source = pl.ds(at + block * MAIN, MAIN)
                target = (pl.ds(chunk * SLOTS, MAIN), pl.ds(block * cut, cut))
                x_rows[target] = jnp.where(first, here[source, :], there[source, :])
                q_rows[target] = jnp.where(first, there[source, :], here[source, :])
            source = pl.ds(at + BLOCKS * MAIN, BLOCKS * REST)
            here_rest = dot(places, here[source, :]).astype(BF16)
            there_rest = dot(places, there[source, :]).astype(BF16)
            for block in range(BLOCKS):
                rows = slice(block * 16, block * 16 + 16)
                target = (pl.ds(chunk * SLOTS + MAIN, 16), pl.ds(block * cut, cut))
                x_rows[target] = jnp.where(first, here_rest[rows], there_rest[rows])
                q_rows[target] = jnp.where(first, there_rest[rows], here_rest[rows])
            chunk += 1


def activations(x_rows, q_rows, w_gate, w_up, w_down):
    gate_pre = dot(w_gate[...], x_rows[...], 1, 1)
    up_pre = dot(w_up[...], x_rows[...], 1, 1)
    hidden_grad = dot(w_down[...], q_rows[...], 1, 1)
    gate_sig = jax.nn.sigmoid(gate_pre)
    gate_act = gate_pre * gate_sig
    hidden = (gate_act * up_pre).astype(BF16)
    gate_grad = (hidden_grad * up_pre * gate_sig * (1.0 + gate_pre * (1.0 - gate_sig))).astype(BF16)
    up_grad = (hidden_grad * gate_act).astype(BF16)
    return gate_grad, up_grad, hidden


def own_kernel(experts, pieces, frag_ref, *refs):
    mine, theirs = refs[:pieces], refs[pieces : 2 * pieces]
    w_gate, w_up, w_down = refs[2 * pieces : 2 * pieces + 3]
    outs = refs[2 * pieces + 3 : 2 * pieces + 6]
    frag_out, load_out, x_rows, q_rows, stage, sems = refs[2 * pieces + 6 :]
    join(mine, theirs, x_rows, q_rows)
    total = jnp.zeros((1, 128), F32)
    for step in range(experts):
        full = x_rows[pl.ds(step * SLOTS, SLOTS), pl.ds(0, 128)].astype(F32) < EMPTY / 2
        valid = lax.broadcasted_iota(jnp.int32, full.shape, 0) < CAP
        total += jnp.sum(jnp.where(full & valid, 1.0, 0.0), axis=0, keepdims=True)
    load_out[...] = total / (experts * CAP)
    acts = activations(x_rows, q_rows, w_gate, w_up, w_down)
    cut = frag_out.shape[2]
    frag_columns = pl.ds(pl.multiple_of(frag_ref[0] * cut, cut), cut)
    copies = []
    for piece, (act, rows, out) in enumerate(zip(acts, (x_rows, x_rows, q_rows), outs)):
        for at in range(FRAGS):
            columns = pl.ds(at * cut, cut)
            stage[piece, :, columns] = dot(act, rows[:, columns]).astype(BF16)
        copies.append(pltpu.make_async_copy(stage.at[piece], out, sems.at[piece]))
        copies[-1].start()
    for piece, (act, rows) in enumerate(zip(acts, (x_rows, x_rows, q_rows))):
        frag_out[piece] = dot(act, rows[:, frag_columns])
    for copy in copies:
        copy.wait()


def own(experts, fragment, mine, theirs, weights):
    units, width = weights[0].shape
    cut = width // FRAGS
    pieces = len(mine)
    return pl.pallas_call(
        functools.partial(own_kernel, experts, pieces),
        out_shape=[jax.ShapeDtypeStruct((units, width), BF16)] * 3
        + [pltpu.VMEM((3, units, cut), F32), jax.ShapeDtypeStruct((1, 128), F32)],
        in_specs=[SMEM] + [VMEM] * (2 * pieces + 3),
        out_specs=[HBM] * 3 + [VMEM] * 2,
        scratch_shapes=[pltpu.VMEM((experts * SLOTS, width), BF16)] * 2
        + [pltpu.VMEM((3, units, width), BF16), pltpu.SemaphoreType.DMA((3,))],
        name="own",
        compiler_params=pltpu.CompilerParams(vmem_limit_bytes=32 << 20),
        cost_estimate=pl.CostEstimate(
            flops=12 * units * width * experts * SLOTS, bytes_accessed=12 * units * width, transcendentals=0
        ),
    )(fragment, *mine, *theirs, *weights)


def other_kernel(pieces, frag_ref, *refs):
    mine, theirs = refs[:pieces], refs[pieces : 2 * pieces]
    w_gate, w_up, w_down = refs[2 * pieces : 2 * pieces + 3]
    frag_in = refs[2 * pieces + 3]
    outs = refs[2 * pieces + 7 : 2 * pieces + 10]
    x_rows, q_rows, cuts, sems = refs[2 * pieces + 10 :]
    join(mine, theirs, x_rows, q_rows)
    acts = activations(x_rows, q_rows, w_gate, w_up, w_down)
    cut = frag_in.shape[2]
    columns = pl.ds(pl.multiple_of(frag_ref[0] * cut, cut), cut)
    copies = []
    for piece, (act, rows) in enumerate(zip(acts, (x_rows, x_rows, q_rows))):
        grad = dot(act, rows[:, columns])
        cuts[piece] = ((frag_in[piece] + grad) * 0.5).astype(BF16)
        copies.append(
            pltpu.make_async_copy(cuts.at[piece], outs[piece].at[:, columns], sems.at[piece])
        )
        copies[-1].start()
    for copy in copies:
        copy.wait()


def other(fragment, mine, theirs, weights, frag_grad, grads):
    units, width = weights[0].shape
    cut = width // FRAGS
    pieces = len(mine)
    rows = sum(part.shape[0] for part in mine) // (BLOCKS * CAP) * SLOTS
    at = 1 + 2 * pieces + 4
    return pl.pallas_call(
        functools.partial(other_kernel, pieces),
        out_shape=[jax.ShapeDtypeStruct((units, width), BF16)] * 3,
        in_specs=[SMEM] + [VMEM] * (2 * pieces + 4) + [ANY] * 3,
        out_specs=[ANY] * 3,
        scratch_shapes=[pltpu.VMEM((rows, width), BF16)] * 2
        + [pltpu.VMEM((3, units, cut), BF16), pltpu.SemaphoreType.DMA((3,))],
        input_output_aliases={at: 0, at + 1: 1, at + 2: 2},
        name="other",
        compiler_params=pltpu.CompilerParams(vmem_limit_bytes=32 << 20),
        cost_estimate=pl.CostEstimate(
            flops=8 * units * width * rows, bytes_accessed=8 * units * width, transcendentals=0
        ),
    )(fragment, *mine, *theirs, *weights, frag_grad, *grads)


def send(array, axis, step):
    size = lax.axis_size(axis)
    return lax.ppermute(array, axis, [(index, peer(index, step, size)) for index in range(size)])


def tie(*arrays):
    return lax.optimization_barrier(arrays)


def two_replicas(fragment, packed, weights):
    r0 = packed[0]
    r3 = send(packed[3], "expert", 3)
    x0 = send(r0, "replica", 1)
    r1 = send(packed[1], "expert", 1)
    x1 = send(packed[1], ("expert", "replica"), 3)
    r2 = send(packed[2], "expert", 2)
    weights = load(weights, fragment, r0)
    r3, x0, *weights = tie(r3, x0, *weights)
    x3 = send(r3, "replica", 1)
    r2, x3, r1, x1 = tie(r2, x3, r1, x1)
    x2 = send(r2, "replica", 1)
    near = stack([r0, r1, r3, r2])
    c0 = send(near, "tensor", 1)
    far = stack([x0, x1, x3])
    f0 = send(far, "tensor", 1)
    mine, theirs = [near], [c0]
    *grads, frag_grad, filled = own(4, fragment, mine, theirs, weights)
    x2, filled = tie(x2, filled)
    f3 = send(x2, "tensor", 1)
    grads = other(fragment, [far, x2], [f0, f3], weights, frag_grad, grads)
    return grads, filled


def any_replicas(experts, replicas, fragment, packed, weights):
    mine = [packed[0]] + [send(packed[step], "expert", step) for step in range(1, experts)]
    theirs = [send(rows, "tensor", 1) for rows in mine]
    *grads, frag_grad, filled = own(experts, fragment, mine, theirs, weights)
    synced = lax.psum(frag_grad.astype(BF16), "replica").astype(F32)
    begin = fragment[0] * (weights[0].shape[1] // FRAGS)
    grads = [
        lax.dynamic_update_slice_in_dim(grad, (piece / replicas).astype(BF16), begin, 1)
        for grad, piece in zip(grads, synced)
    ]
    return grads, filled


def per_device(tokens, out_grad, expert_ids, route_weight, gate_proj, up_proj, down_proj, fragment):
    experts = lax.axis_size("expert")
    replicas = lax.axis_size("replica")
    weights = (gate_proj[0], up_proj[0], down_proj[0])
    packed = pack(experts, tokens[0], out_grad[0], expert_ids[0], route_weight[0])
    if replicas == 2 and experts == 4:
        grads, filled = two_replicas(fragment, packed, weights)
    else:
        grads, filled = any_replicas(experts, replicas, fragment, packed, weights)
    return tuple(grad[None, None] for grad in grads) + (filled[:, :1],)


def solution(mesh):
    rows = P(("group", "replica"), "expert", None)
    units = P("expert", "tensor", None)
    grad = P(("group", "replica"), "expert", "tensor", None)
    return jax.shard_map(
        per_device,
        mesh=mesh,
        in_specs=(rows, rows, rows, rows, units, units, units, P("group")),
        out_specs=(grad, grad, grad, P(("group", "replica"), "expert")),
        check_vma=False,
    )
```

```python
import functools

import jax
import jax.numpy as jnp
from jax import lax
from jax.experimental import pallas as pl
from jax.experimental.pallas import tpu as pltpu
from jax.sharding import PartitionSpec as P

FRAGS = 4
CAP = 60
SLOTS = 64
BLOCKS = 4
MAIN = CAP // 16 * 16
REST = CAP - MAIN
EMPTY = 64.0
F32 = jnp.float32
BF16 = jnp.bfloat16
VMEM = pl.BlockSpec(memory_space=pltpu.VMEM)
SMEM = pl.BlockSpec(memory_space=pltpu.SMEM)
ANY = pl.BlockSpec(memory_space=pl.ANY)
HBM = pl.BlockSpec(memory_space=pltpu.HBM)


def dot(left, right, left_dim=1, right_dim=0):
    return lax.dot_general(
        left, right, (((left_dim,), (right_dim,)), ((), ())), preferred_element_type=F32
    )


def peer(index, step, size):
    return index ^ step if size & (size - 1) == 0 else (index + step) % size


def pack_kernel(experts, tok_hbm, grad_hbm, ids_hbm, weight_hbm, *refs):
    *out_refs, source_ref, ids_ref, weight_ref, sems = refs
    me = lax.axis_index("expert")
    first = lax.axis_index("tensor") == 0
    tokens = ids_ref.shape[1]
    ids_copy = pltpu.make_async_copy(ids_hbm, ids_ref, sems.at[0])
    weight_copy = pltpu.make_async_copy(weight_hbm, weight_ref, sems.at[1])
    ids_copy.start()
    weight_copy.start()
    cut = source_ref.shape[1] // BLOCKS
    tok_copy = pltpu.make_async_copy(tok_hbm, source_ref, sems.at[2])
    grad_copy = pltpu.make_async_copy(grad_hbm, source_ref, sems.at[2])

    @pl.when(first)
    def _():
        tok_copy.start()

    @pl.when(jnp.logical_not(first))
    def _():
        grad_copy.start()

    ids_copy.wait()
    weight_copy.wait()
    ids = ids_ref[...]
    weight = weight_ref[...]
    members, weights = [], []
    for step in range(experts):
        match = ids == peer(me, step, experts)
        members.append(jnp.max(jnp.where(match, 1.0, 0.0), axis=0, keepdims=True))
        weights.append(jnp.sum(jnp.where(match, weight, 0.0), axis=0, keepdims=True))
    member = jnp.concatenate(members, axis=0)
    earlier = (
        lax.broadcasted_iota(jnp.int32, (tokens, tokens), 0)
        < lax.broadcasted_iota(jnp.int32, (tokens, tokens), 1)
    ).astype(F32).astype(BF16)
    position = dot(member.astype(BF16), earlier)
    slot = lax.broadcasted_iota(jnp.int32, (SLOTS, tokens), 0).astype(F32)
    rows = lax.broadcasted_iota(jnp.int32, (SLOTS, 1), 0).astype(F32)
    picks, scales, fills = [], [], []
    for step in range(experts):
        hit = (slot == position[step : step + 1, :]) & (member[step : step + 1, :] > 0.5)
        pick = jnp.where(hit, 1.0, 0.0)
        scale = jnp.sum(pick * weights[step], axis=1, keepdims=True)
        scales.append(jnp.where(first, 1.0, scale))
        count = jnp.sum(members[step], axis=1, keepdims=True)
        fills.append(jnp.where((rows >= count) & first, EMPTY, 0.0))
        picks.append(pick.astype(BF16))
    picks = jnp.concatenate(picks, axis=0)
    scales = jnp.concatenate(scales, axis=0)
    fills = jnp.concatenate(fills, axis=0)
    places = rest_places((BLOCKS * REST, BLOCKS * 16), 0, 1)
    tok_copy.wait()
    packed = (dot(picks, source_ref[...]) * scales + fills).astype(BF16)
    rests = []
    for block in range(BLOCKS):
        for step in range(experts):
            tile = packed[step * SLOTS : (step + 1) * SLOTS, block * cut : (block + 1) * cut]
            out_refs[step][pl.ds(block * MAIN, MAIN), :] = tile[:MAIN]
            rests.append(tile[MAIN:])
    for step in range(experts):
        rest = dot(places, jnp.concatenate(rests[step::experts], axis=0))
        out_refs[step][pl.ds(BLOCKS * MAIN, BLOCKS * REST), :] = rest.astype(BF16)
        more = out_refs[step].shape[0] - BLOCKS * CAP
        if more:
            out_refs[step][pl.ds(BLOCKS * CAP, more), :] = jnp.zeros((more, cut), BF16)


def rest_places(shape, wire, block):
    left = lax.broadcasted_iota(jnp.int32, shape, wire)
    right = lax.broadcasted_iota(jnp.int32, shape, block)
    hit = (lax.rem(right, 16) < REST) & (left == right // 16 * REST + lax.rem(right, 16))
    return hit.astype(F32).astype(BF16)


def in_hbm(array):
    return pltpu.with_memory_space_constraint(array, pltpu.HBM)


def load_kernel(count, *refs):
    sources, targets, sems = refs[:count], refs[count + 2 : 2 * count + 2], refs[-1]
    copies = [
        pltpu.make_async_copy(source, target, sems.at[index])
        for index, (source, target) in enumerate(zip(sources, targets))
    ]
    for copy in copies:
        copy.start()
    for copy in copies:
        copy.wait()


def load(arrays, fragment, after):
    count = len(arrays)
    return pl.pallas_call(
        functools.partial(load_kernel, count),
        out_shape=[pltpu.VMEM(array.shape, array.dtype) for array in arrays],
        in_specs=[HBM] * count + [SMEM, ANY],
        out_specs=[VMEM] * count,
        scratch_shapes=[pltpu.SemaphoreType.DMA((count,))],
        compiler_params=pltpu.CompilerParams(vmem_limit_bytes=8 << 20),
        name="load",
    )(*[in_hbm(array) for array in arrays], fragment, after)


def stack_kernel(*refs):
    *parts, whole = refs
    for step, part in enumerate(parts):
        whole[pl.ds(step * BLOCKS * CAP, BLOCKS * CAP), :] = part[pl.ds(0, BLOCKS * CAP), :]


def stack(parts):
    rows = len(parts) * BLOCKS * CAP
    return pl.pallas_call(
        stack_kernel,
        out_shape=pltpu.VMEM((rows, parts[0].shape[1]), parts[0].dtype),
        in_specs=[VMEM] * len(parts),
        out_specs=VMEM,
        compiler_params=pltpu.CompilerParams(vmem_limit_bytes=8 << 20),
        name="stack",
    )(*parts)


def pack(rows, tokens, out_grad, ids, weight):
    width = tokens.shape[1]
    inputs = [in_hbm(array) for array in (tokens, out_grad, ids.T, weight.T)]
    return pl.pallas_call(
        functools.partial(pack_kernel, len(rows)),
        out_shape=[pltpu.VMEM((count, width // BLOCKS), BF16) for count in rows],
        in_specs=[HBM] * 4,
        out_specs=[VMEM] * len(rows),
        scratch_shapes=[
            pltpu.VMEM((tokens.shape[0], width), BF16),
            pltpu.VMEM(ids.shape[::-1], jnp.int32),
            pltpu.VMEM(ids.shape[::-1], F32),
            pltpu.SemaphoreType.DMA((3,)),
        ],
        name="pack",
        compiler_params=pltpu.CompilerParams(vmem_limit_bytes=16 << 20),
    )(*inputs)


def join(parts, x_rows, q_rows):
    first = lax.axis_index("tensor") == 0
    cut = x_rows.shape[1] // BLOCKS
    places = rest_places((BLOCKS * 16, BLOCKS * REST), 1, 0)
    row = 0
    for here, there, begin, count in parts:
        for at in range(begin * BLOCKS * CAP, (begin + count) * BLOCKS * CAP, BLOCKS * CAP):
            for block in range(BLOCKS):
                source = pl.ds(at + block * MAIN, MAIN)
                target = (pl.ds(row, MAIN), pl.ds(block * cut, cut))
                x_rows[target] = jnp.where(first, here[source, :], there[source, :])
                q_rows[target] = jnp.where(first, there[source, :], here[source, :])
            source = pl.ds(at + BLOCKS * MAIN, BLOCKS * REST)
            here_rest = dot(places, here[source, :]).astype(BF16)
            there_rest = dot(places, there[source, :]).astype(BF16)
            for block in range(BLOCKS):
                rest = slice(block * 16, block * 16 + 16)
                target = (pl.ds(row + MAIN, 16), pl.ds(block * cut, cut))
                x_rows[target] = jnp.where(first, here_rest[rest], there_rest[rest])
                q_rows[target] = jnp.where(first, there_rest[rest], here_rest[rest])
            row += SLOTS


def activations(x_rows, q_rows, w_gate, w_up, w_down):
    gate_pre = dot(w_gate[...], x_rows[...], 1, 1)
    up_pre = dot(w_up[...], x_rows[...], 1, 1)
    hidden_grad = dot(w_down[...], q_rows[...], 1, 1)
    gate_sig = jax.nn.sigmoid(gate_pre)
    gate_act = gate_pre * gate_sig
    hidden = (gate_act * up_pre).astype(BF16)
    gate_grad = (hidden_grad * up_pre * gate_sig * (1.0 + gate_pre * (1.0 - gate_sig))).astype(BF16)
    up_grad = (hidden_grad * gate_act).astype(BF16)
    return gate_grad, up_grad, hidden


def own_kernel(experts, frag_ref, mine, theirs, w_gate, w_up, w_down, *refs):
    grads, frag_out, load_out, x_rows, q_rows = refs
    join([(mine, theirs, 0, experts)], x_rows, q_rows)
    total = jnp.zeros((1, 128), F32)
    for step in range(experts):
        full = x_rows[pl.ds(step * SLOTS, SLOTS), pl.ds(0, 128)].astype(F32) < EMPTY / 2
        valid = lax.broadcasted_iota(jnp.int32, full.shape, 0) < CAP
        total += jnp.sum(jnp.where(full & valid, 1.0, 0.0), axis=0, keepdims=True)
    load_out[...] = total / (experts * CAP)
    acts = activations(x_rows, q_rows, w_gate, w_up, w_down)
    cut = frag_out.shape[2]
    frag_columns = pl.ds(pl.multiple_of(frag_ref[0] * cut, cut), cut)
    for piece, (act, rows) in enumerate(zip(acts, (x_rows, x_rows, q_rows))):
        grads[piece] = dot(act, rows[...]).astype(BF16)
        frag_out[piece] = dot(act, rows[:, frag_columns])


def own(experts, fragment, mine, theirs, weights):
    units, width = weights[0].shape
    cut = width // FRAGS
    rows = experts * SLOTS
    return pl.pallas_call(
        functools.partial(own_kernel, experts),
        out_shape=[
            pltpu.VMEM((3, units, width), BF16),
            pltpu.VMEM((3, units, cut), F32),
            jax.ShapeDtypeStruct((1, 128), F32),
        ],
        in_specs=[SMEM] + [VMEM] * 5,
        out_specs=[VMEM] * 3,
        scratch_shapes=[pltpu.VMEM((rows, width), BF16)] * 2,
        name="own",
        compiler_params=pltpu.CompilerParams(vmem_limit_bytes=24 << 20),
        cost_estimate=pl.CostEstimate(
            flops=12 * units * width * rows, bytes_accessed=12 * units * width, transcendentals=0
        ),
    )(fragment, mine, theirs, *weights)


def other_kernel(ranges, frag_ref, *refs):
    pieces = len(ranges)
    mine, theirs = refs[:pieces], refs[pieces : 2 * pieces]
    w_gate, w_up, w_down, grads, frag_in = refs[2 * pieces : 2 * pieces + 5]
    outs = refs[2 * pieces + 5 : 2 * pieces + 8]
    x_rows, q_rows, cuts, sems = refs[2 * pieces + 8 :]
    cut = frag_in.shape[2]
    frag = frag_ref[0]
    copies = []
    for piece, out in enumerate(outs):
        for step in range(1, FRAGS):
            block = lax.rem(frag + step, FRAGS)
            columns = pl.ds(pl.multiple_of(block * cut, cut), cut)
            copies.append(
                pltpu.make_async_copy(
                    grads.at[piece, :, columns], out.at[:, columns], sems.at[piece, step]
                )
            )
            copies[-1].start()
    join([(*pair, *span) for *pair, span in zip(mine, theirs, ranges)], x_rows, q_rows)
    acts = activations(x_rows, q_rows, w_gate, w_up, w_down)
    columns = pl.ds(pl.multiple_of(frag * cut, cut), cut)
    for piece, (act, rows) in enumerate(zip(acts, (x_rows, x_rows, q_rows))):
        grad = dot(act, rows[:, columns])
        cuts[piece] = ((frag_in[piece] + grad) * 0.5).astype(BF16)
        copies.append(
            pltpu.make_async_copy(cuts.at[piece], outs[piece].at[:, columns], sems.at[piece, 0])
        )
        copies[-1].start()
    for copy in copies:
        copy.wait()


def other(fragment, mine, theirs, ranges, weights, grads, frag_grad):
    units, width = weights[0].shape
    cut = width // FRAGS
    pieces = len(mine)
    rows = sum(count for _, count in ranges) * SLOTS
    return pl.pallas_call(
        functools.partial(other_kernel, ranges),
        out_shape=[jax.ShapeDtypeStruct((units, width), BF16)] * 3,
        in_specs=[SMEM] + [VMEM] * (2 * pieces + 5),
        out_specs=[HBM] * 3,
        scratch_shapes=[pltpu.VMEM((rows, width), BF16)] * 2
        + [pltpu.VMEM((3, units, cut), BF16), pltpu.SemaphoreType.DMA((3, FRAGS))],
        name="other",
        compiler_params=pltpu.CompilerParams(vmem_limit_bytes=24 << 20),
        cost_estimate=pl.CostEstimate(
            flops=8 * units * width * rows, bytes_accessed=8 * units * width, transcendentals=0
        ),
    )(fragment, *mine, *theirs, *weights, grads, frag_grad)


def send(array, axis, step):
    size = lax.axis_size(axis)
    return lax.ppermute(array, axis, [(index, peer(index, step, size)) for index in range(size)])


def tie(*arrays):
    return lax.optimization_barrier(arrays)


def two_replicas(fragment, packed, weights):
    r0 = packed[0]
    r3 = send(packed[3], "expert", 3)
    x0 = send(r0, "replica", 1)
    r1 = send(packed[1], "expert", 1)
    x1 = send(packed[1], ("expert", "replica"), 3)
    r2 = send(packed[2], "expert", 2)
    weights = load(weights, fragment, r0)
    r3, *weights = tie(r3, *weights)
    x3 = send(r3, "replica", 1)
    x2 = send(r2, "replica", 1)
    r1, x1, x3, x0 = tie(r1, x1, x3, x0)
    near = stack([r0, r1, r2, r3])
    c0 = send(near, "tensor", 1)
    far = stack([x0, x1, x2, x3])
    f0 = send(far, "tensor", 1)
    grads, frag_grad, filled = own(4, fragment, near, c0, weights)
    grads = other(fragment, [far], [f0], [(0, 4)], weights, grads, frag_grad)
    return grads, filled


def any_replicas(experts, replicas, fragment, packed, weights):
    mine = [packed[0]] + [send(packed[step], "expert", step) for step in range(1, experts)]
    mine = stack(mine)
    theirs = send(mine, "tensor", 1)
    grads, frag_grad, filled = own(experts, fragment, mine, theirs, weights)
    synced = lax.psum(frag_grad.astype(BF16), "replica").astype(F32)
    begin = fragment[0] * synced.shape[2]
    grads = [
        lax.dynamic_update_slice_in_dim(grad, (piece / replicas).astype(BF16), begin, 1)
        for grad, piece in zip(grads, synced)
    ]
    return grads, filled


def per_device(tokens, out_grad, expert_ids, route_weight, gate_proj, up_proj, down_proj, fragment):
    experts = lax.axis_size("expert")
    replicas = lax.axis_size("replica")
    weights = (gate_proj[0], up_proj[0], down_proj[0])
    rows = [BLOCKS * CAP] * experts
    if replicas == 2 and experts == 4:
        rows[2] += 16
    packed = pack(rows, tokens[0], out_grad[0], expert_ids[0], route_weight[0])
    if replicas == 2 and experts == 4:
        grads, filled = two_replicas(fragment, packed, weights)
    else:
        grads, filled = any_replicas(experts, replicas, fragment, packed, weights)
    return tuple(grad[None, None] for grad in grads) + (filled[:, :1],)


def solution(mesh):
    rows = P(("group", "replica"), "expert", None)
    units = P("expert", "tensor", None)
    grad = P(("group", "replica"), "expert", "tensor", None)
    return jax.shard_map(
        per_device,
        mesh=mesh,
        in_specs=(rows, rows, rows, rows, units, units, units, P("group")),
        out_specs=(grad, grad, grad, P(("group", "replica"), "expert")),
        check_vma=False,
    )
```

```python
import functools

import jax
import jax.numpy as jnp
from jax import lax
from jax.experimental import pallas as pl
from jax.experimental.pallas import tpu as pltpu
from jax.sharding import PartitionSpec as P

FRAGS = 4
CAP = 60
SLOTS = 64
BLOCKS = 4
MAIN = CAP // 16 * 16
REST = CAP - MAIN
EMPTY = 64.0
F32 = jnp.float32
BF16 = jnp.bfloat16
VMEM = pl.BlockSpec(memory_space=pltpu.VMEM)
SMEM = pl.BlockSpec(memory_space=pltpu.SMEM)
ANY = pl.BlockSpec(memory_space=pl.ANY)
HBM = pl.BlockSpec(memory_space=pltpu.HBM)


def dot(left, right, left_dim=1, right_dim=0):
    return lax.dot_general(
        left, right, (((left_dim,), (right_dim,)), ((), ())), preferred_element_type=F32
    )


def peer(index, step, size):
    return index ^ step if size & (size - 1) == 0 else (index + step) % size


def pack_kernel(experts, tok_hbm, grad_hbm, ids_hbm, weight_hbm, *refs):
    *out_refs, source_ref, ids_ref, weight_ref, sems = refs
    me = lax.axis_index("expert")
    first = lax.axis_index("tensor") == 0
    tokens = ids_ref.shape[1]
    ids_copy = pltpu.make_async_copy(ids_hbm, ids_ref, sems.at[0])
    weight_copy = pltpu.make_async_copy(weight_hbm, weight_ref, sems.at[1])
    ids_copy.start()
    weight_copy.start()
    cut = source_ref.shape[1] // BLOCKS
    tok_copy = pltpu.make_async_copy(tok_hbm, source_ref, sems.at[2])
    grad_copy = pltpu.make_async_copy(grad_hbm, source_ref, sems.at[2])

    @pl.when(first)
    def _():
        tok_copy.start()

    @pl.when(jnp.logical_not(first))
    def _():
        grad_copy.start()

    ids_copy.wait()
    weight_copy.wait()
    ids = ids_ref[...]
    weight = weight_ref[...]
    members, weights = [], []
    for step in range(experts):
        match = ids == peer(me, step, experts)
        members.append(jnp.max(jnp.where(match, 1.0, 0.0), axis=0, keepdims=True))
        weights.append(jnp.sum(jnp.where(match, weight, 0.0), axis=0, keepdims=True))
    member = jnp.concatenate(members, axis=0)
    earlier = (
        lax.broadcasted_iota(jnp.int32, (tokens, tokens), 0)
        < lax.broadcasted_iota(jnp.int32, (tokens, tokens), 1)
    ).astype(F32).astype(BF16)
    position = dot(member.astype(BF16), earlier)
    slot = lax.broadcasted_iota(jnp.int32, (SLOTS, tokens), 0).astype(F32)
    rows = lax.broadcasted_iota(jnp.int32, (SLOTS, 1), 0).astype(F32)
    picks, scales, fills = [], [], []
    for step in range(experts):
        hit = (slot == position[step : step + 1, :]) & (member[step : step + 1, :] > 0.5)
        pick = jnp.where(hit, 1.0, 0.0)
        scale = jnp.sum(pick * weights[step], axis=1, keepdims=True)
        scales.append(jnp.where(first, 1.0, scale))
        count = jnp.sum(members[step], axis=1, keepdims=True)
        fills.append(jnp.where((rows >= count) & first, EMPTY, 0.0))
        picks.append(pick.astype(BF16))
    picks = jnp.concatenate(picks, axis=0)
    scales = jnp.concatenate(scales, axis=0)
    fills = jnp.concatenate(fills, axis=0)
    places = rest_places((BLOCKS * REST, BLOCKS * 16), 0, 1)
    tok_copy.wait()
    packed = (dot(picks, source_ref[...]) * scales + fills).astype(BF16)
    rests = []
    for block in range(BLOCKS):
        for step in range(experts):
            tile = packed[step * SLOTS : (step + 1) * SLOTS, block * cut : (block + 1) * cut]
            out_refs[step][pl.ds(block * MAIN, MAIN), :] = tile[:MAIN]
            rests.append(tile[MAIN:])
    for step in range(experts):
        rest = dot(places, jnp.concatenate(rests[step::experts], axis=0))
        out_refs[step][pl.ds(BLOCKS * MAIN, BLOCKS * REST), :] = rest.astype(BF16)


def rest_places(shape, wire, block):
    left = lax.broadcasted_iota(jnp.int32, shape, wire)
    right = lax.broadcasted_iota(jnp.int32, shape, block)
    hit = (lax.rem(right, 16) < REST) & (left == right // 16 * REST + lax.rem(right, 16))
    return hit.astype(F32).astype(BF16)


def in_hbm(array):
    return pltpu.with_memory_space_constraint(array, pltpu.HBM)


def load_kernel(count, *refs):
    sources, targets, sems = refs[:count], refs[count + 2 : 2 * count + 2], refs[-1]
    copies = [
        pltpu.make_async_copy(source, target, sems.at[index])
        for index, (source, target) in enumerate(zip(sources, targets))
    ]
    for copy in copies:
        copy.start()
    for copy in copies:
        copy.wait()


def load(arrays, fragment, after):
    count = len(arrays)
    return pl.pallas_call(
        functools.partial(load_kernel, count),
        out_shape=[pltpu.VMEM(array.shape, array.dtype) for array in arrays],
        in_specs=[HBM] * count + [SMEM, ANY],
        out_specs=[VMEM] * count,
        scratch_shapes=[pltpu.SemaphoreType.DMA((count,))],
        compiler_params=pltpu.CompilerParams(vmem_limit_bytes=8 << 20),
        name="load",
    )(*[in_hbm(array) for array in arrays], fragment, after)


def stack_kernel(*refs):
    *parts, whole = refs
    at = 0
    for part in parts:
        whole[pl.ds(at, part.shape[0]), :] = part[...]
        at += part.shape[0]


def stack(parts):
    rows = sum(part.shape[0] for part in parts)
    return pl.pallas_call(
        stack_kernel,
        out_shape=pltpu.VMEM((rows, parts[0].shape[1]), parts[0].dtype),
        in_specs=[VMEM] * len(parts),
        out_specs=VMEM,
        compiler_params=pltpu.CompilerParams(vmem_limit_bytes=8 << 20),
        name="stack",
    )(*parts)


def pack(experts, tokens, out_grad, ids, weight):
    width = tokens.shape[1]
    inputs = [in_hbm(array) for array in (tokens, out_grad, ids.T, weight.T)]
    return pl.pallas_call(
        functools.partial(pack_kernel, experts),
        out_shape=[pltpu.VMEM((BLOCKS * CAP, width // BLOCKS), BF16)] * experts,
        in_specs=[HBM] * 4,
        out_specs=[VMEM] * experts,
        scratch_shapes=[
            pltpu.VMEM((tokens.shape[0], width), BF16),
            pltpu.VMEM(ids.shape[::-1], jnp.int32),
            pltpu.VMEM(ids.shape[::-1], F32),
            pltpu.SemaphoreType.DMA((3,)),
        ],
        name="pack",
        compiler_params=pltpu.CompilerParams(vmem_limit_bytes=16 << 20),
    )(*inputs)


def join(parts, x_rows, q_rows):
    first = lax.axis_index("tensor") == 0
    cut = x_rows.shape[1] // BLOCKS
    places = rest_places((BLOCKS * 16, BLOCKS * REST), 1, 0)
    row = 0
    for here, there, begin, count in parts:
        for at in range(begin * BLOCKS * CAP, (begin + count) * BLOCKS * CAP, BLOCKS * CAP):
            for block in range(BLOCKS):
                source = pl.ds(at + block * MAIN, MAIN)
                target = (pl.ds(row, MAIN), pl.ds(block * cut, cut))
                x_rows[target] = jnp.where(first, here[source, :], there[source, :])
                q_rows[target] = jnp.where(first, there[source, :], here[source, :])
            source = pl.ds(at + BLOCKS * MAIN, BLOCKS * REST)
            here_rest = dot(places, here[source, :]).astype(BF16)
            there_rest = dot(places, there[source, :]).astype(BF16)
            for block in range(BLOCKS):
                rest = slice(block * 16, block * 16 + 16)
                target = (pl.ds(row + MAIN, 16), pl.ds(block * cut, cut))
                x_rows[target] = jnp.where(first, here_rest[rest], there_rest[rest])
                q_rows[target] = jnp.where(first, there_rest[rest], here_rest[rest])
            row += SLOTS


def activations(x_rows, q_rows, w_gate, w_up, w_down):
    gate_pre = dot(w_gate[...], x_rows[...], 1, 1)
    up_pre = dot(w_up[...], x_rows[...], 1, 1)
    hidden_grad = dot(w_down[...], q_rows[...], 1, 1)
    gate_sig = jax.nn.sigmoid(gate_pre)
    gate_act = gate_pre * gate_sig
    hidden = (gate_act * up_pre).astype(BF16)
    gate_grad = (hidden_grad * up_pre * gate_sig * (1.0 + gate_pre * (1.0 - gate_sig))).astype(BF16)
    up_grad = (hidden_grad * gate_act).astype(BF16)
    return gate_grad, up_grad, hidden


def own_kernel(experts, frag_ref, mine, theirs, w_gate, w_up, w_down, *refs):
    grads, acts, x_rows, q_rows, load_out = refs
    join([(mine, theirs, 0, experts)], x_rows, q_rows)
    for piece, act in enumerate(activations(x_rows, q_rows, w_gate, w_up, w_down)):
        acts[piece] = act
    for piece, rows in enumerate((x_rows, x_rows, q_rows)):
        grads[piece] = dot(acts[piece], rows[...]).astype(BF16)
    total = jnp.zeros((1, 128), F32)
    for step in range(experts):
        full = x_rows[pl.ds(step * SLOTS, SLOTS), pl.ds(0, 128)].astype(F32) < EMPTY / 2
        valid = lax.broadcasted_iota(jnp.int32, full.shape, 0) < CAP
        total += jnp.sum(jnp.where(full & valid, 1.0, 0.0), axis=0, keepdims=True)
    load_out[...] = total / (experts * CAP)


def own(experts, fragment, mine, theirs, weights):
    units, width = weights[0].shape
    rows = experts * SLOTS
    return pl.pallas_call(
        functools.partial(own_kernel, experts),
        out_shape=[
            pltpu.VMEM((3, units, width), BF16),
            pltpu.VMEM((3, units, rows), BF16),
            pltpu.VMEM((rows, width), BF16),
            pltpu.VMEM((rows, width), BF16),
            jax.ShapeDtypeStruct((1, 128), F32),
        ],
        in_specs=[SMEM] + [VMEM] * 5,
        out_specs=[VMEM] * 5,
        name="own",
        compiler_params=pltpu.CompilerParams(vmem_limit_bytes=24 << 20),
        cost_estimate=pl.CostEstimate(
            flops=12 * units * width * rows, bytes_accessed=12 * units * width, transcendentals=0
        ),
    )(fragment, mine, theirs, *weights)


def other_kernel(chunks, frag_ref, mine, theirs, w_gate, w_up, w_down, *refs):
    grads, own_acts, own_x, own_q, *outs, x_rows, q_rows, cuts, sems = refs
    cut = cuts.shape[2]
    frag = frag_ref[0]
    copies = []
    for piece in range(3):
        for step in range(1, FRAGS):
            block = lax.rem(frag + step, FRAGS)
            columns = pl.ds(pl.multiple_of(block * cut, cut), cut)
            copies.append(
                pltpu.make_async_copy(
                    grads.at[piece, :, columns], outs[piece].at[:, columns], sems.at[piece, step]
                )
            )
            copies[-1].start()
    join([(mine, theirs, 0, chunks)], x_rows, q_rows)
    acts = activations(x_rows, q_rows, w_gate, w_up, w_down)
    columns = pl.ds(pl.multiple_of(frag * cut, cut), cut)
    sides = ((own_x, x_rows), (own_x, x_rows), (own_q, q_rows))
    for piece, (here, there) in enumerate(sides):
        grad = dot(own_acts[piece], here[:, columns]) + dot(acts[piece], there[:, columns])
        cuts[piece] = (grad * 0.5).astype(BF16)
        copies.append(
            pltpu.make_async_copy(cuts.at[piece], outs[piece].at[:, columns], sems.at[piece, 0])
        )
        copies[-1].start()
    for copy in copies:
        copy.wait()


def other(chunks, fragment, mine, theirs, weights, parts):
    units, width = weights[0].shape
    cut = width // FRAGS
    rows = chunks * SLOTS
    return pl.pallas_call(
        functools.partial(other_kernel, chunks),
        out_shape=[jax.ShapeDtypeStruct((units, width), BF16)] * 3,
        in_specs=[SMEM] + [VMEM] * 9,
        out_specs=[HBM] * 3,
        scratch_shapes=[pltpu.VMEM((rows, width), BF16)] * 2
        + [pltpu.VMEM((3, units, cut), BF16), pltpu.SemaphoreType.DMA((3, FRAGS))],
        name="other",
        compiler_params=pltpu.CompilerParams(vmem_limit_bytes=24 << 20),
        cost_estimate=pl.CostEstimate(
            flops=8 * units * width * rows, bytes_accessed=8 * units * width, transcendentals=0
        ),
    )(fragment, mine, theirs, *weights, *parts)


def send(array, axis, step):
    size = lax.axis_size(axis)
    return lax.ppermute(array, axis, [(index, peer(index, step, size)) for index in range(size)])


def tie(*arrays):
    return lax.optimization_barrier(arrays)


def two_replicas(fragment, packed, weights):
    r0 = packed[0]
    r3 = send(packed[3], "expert", 3)
    x0 = send(r0, "replica", 1)
    r1 = send(packed[1], "expert", 1)
    x1 = send(packed[1], ("expert", "replica"), 3)
    r2 = send(packed[2], "expert", 2)
    weights = load(weights, fragment, r0)
    r3, *weights = tie(r3, *weights)
    r2, *weights = tie(r2, *weights)
    x3 = send(r3, "replica", 1)
    x2 = send(r2, "replica", 1)
    r1, x1, x3, x0 = tie(r1, x1, x3, x0)
    near = stack([r0, r1, r2, r3])
    c0 = send(near, "tensor", 1)
    far = stack([x0, x1, x2, x3])
    f0 = send(far, "tensor", 1)
    *parts, filled = own(4, fragment, near, c0, weights)
    grads = other(4, fragment, far, f0, weights, parts)
    return grads, filled


def any_replicas(experts, replicas, fragment, packed, weights):
    mine = [packed[0]] + [send(packed[step], "expert", step) for step in range(1, experts)]
    mine = stack(mine)
    theirs = send(mine, "tensor", 1)
    grads, acts, x_rows, q_rows, filled = own(experts, fragment, mine, theirs, weights)
    cut = x_rows.shape[1] // FRAGS
    begin = fragment[0] * cut
    sides = [lax.dynamic_slice_in_dim(rows, begin, cut, 1) for rows in (x_rows, x_rows, q_rows)]
    pieces = jnp.stack([dot(act, side) for act, side in zip(acts, sides)]).astype(BF16)
    synced = lax.psum(pieces, "replica").astype(F32)
    grads = [
        lax.dynamic_update_slice_in_dim(grad, (piece / replicas).astype(BF16), begin, 1)
        for grad, piece in zip(grads, synced)
    ]
    return grads, filled


def per_device(tokens, out_grad, expert_ids, route_weight, gate_proj, up_proj, down_proj, fragment):
    experts = lax.axis_size("expert")
    replicas = lax.axis_size("replica")
    weights = (gate_proj[0], up_proj[0], down_proj[0])
    packed = pack(experts, tokens[0], out_grad[0], expert_ids[0], route_weight[0])
    if replicas == 2 and experts == 4:
        grads, filled = two_replicas(fragment, packed, weights)
    else:
        grads, filled = any_replicas(experts, replicas, fragment, packed, weights)
    return tuple(grad[None, None] for grad in grads) + (filled[:, :1],)


def solution(mesh):
    rows = P(("group", "replica"), "expert", None)
    units = P("expert", "tensor", None)
    grad = P(("group", "replica"), "expert", "tensor", None)
    return jax.shard_map(
        per_device,
        mesh=mesh,
        in_specs=(rows, rows, rows, rows, units, units, units, P("group")),
        out_specs=(grad, grad, grad, P(("group", "replica"), "expert")),
        check_vma=False,
    )
```

```python
import functools

import jax
import jax.numpy as jnp
from jax import lax
from jax.experimental import pallas as pl
from jax.experimental.pallas import tpu as pltpu
from jax.sharding import PartitionSpec as P

FRAGS = 4
CAP = 60
SLOTS = 64
BLOCKS = 4
MAIN = CAP // 16 * 16
REST = CAP - MAIN
EMPTY = 64.0
F32 = jnp.float32
BF16 = jnp.bfloat16
VMEM = pl.BlockSpec(memory_space=pltpu.VMEM)
SMEM = pl.BlockSpec(memory_space=pltpu.SMEM)
ANY = pl.BlockSpec(memory_space=pl.ANY)
HBM = pl.BlockSpec(memory_space=pltpu.HBM)


def dot(left, right, left_dim=1, right_dim=0):
    return lax.dot_general(
        left, right, (((left_dim,), (right_dim,)), ((), ())), preferred_element_type=F32
    )


def peer(index, step, size):
    return index ^ step if size & (size - 1) == 0 else (index + step) % size


def pack_kernel(experts, tok_hbm, grad_hbm, ids_hbm, weight_hbm, *refs):
    *out_refs, source_ref, ids_ref, weight_ref, sems = refs
    me = lax.axis_index("expert")
    first = lax.axis_index("tensor") == 0
    tokens = ids_ref.shape[1]
    ids_copy = pltpu.make_async_copy(ids_hbm, ids_ref, sems.at[0])
    weight_copy = pltpu.make_async_copy(weight_hbm, weight_ref, sems.at[1])
    ids_copy.start()
    weight_copy.start()
    cut = source_ref.shape[1] // BLOCKS
    tok_copy = pltpu.make_async_copy(tok_hbm, source_ref, sems.at[2])
    grad_copy = pltpu.make_async_copy(grad_hbm, source_ref, sems.at[2])

    @pl.when(first)
    def _():
        tok_copy.start()

    @pl.when(jnp.logical_not(first))
    def _():
        grad_copy.start()

    ids_copy.wait()
    weight_copy.wait()
    ids = ids_ref[...]
    weight = weight_ref[...]
    members, weights = [], []
    for step in range(experts):
        match = ids == peer(me, step, experts)
        members.append(jnp.max(jnp.where(match, 1.0, 0.0), axis=0, keepdims=True))
        weights.append(jnp.sum(jnp.where(match, weight, 0.0), axis=0, keepdims=True))
    member = jnp.concatenate(members, axis=0)
    earlier = (
        lax.broadcasted_iota(jnp.int32, (tokens, tokens), 0)
        < lax.broadcasted_iota(jnp.int32, (tokens, tokens), 1)
    ).astype(F32).astype(BF16)
    position = dot(member.astype(BF16), earlier)
    slot = lax.broadcasted_iota(jnp.int32, (SLOTS, tokens), 0).astype(F32)
    rows = lax.broadcasted_iota(jnp.int32, (SLOTS, 1), 0).astype(F32)
    picks, scales, fills = [], [], []
    for step in range(experts):
        hit = (slot == position[step : step + 1, :]) & (member[step : step + 1, :] > 0.5)
        pick = jnp.where(hit, 1.0, 0.0)
        scale = jnp.sum(pick * weights[step], axis=1, keepdims=True)
        scales.append(jnp.where(first, 1.0, scale))
        count = jnp.sum(members[step], axis=1, keepdims=True)
        fills.append(jnp.where((rows >= count) & first, EMPTY, 0.0))
        picks.append(pick.astype(BF16))
    picks = jnp.concatenate(picks, axis=0)
    scales = jnp.concatenate(scales, axis=0)
    fills = jnp.concatenate(fills, axis=0)
    places = rest_places((BLOCKS * REST, BLOCKS * 16), 0, 1)
    tok_copy.wait()
    packed = (dot(picks, source_ref[...]) * scales + fills).astype(BF16)
    rests = []
    for block in range(BLOCKS):
        for step in range(experts):
            tile = packed[step * SLOTS : (step + 1) * SLOTS, block * cut : (block + 1) * cut]
            out_refs[step][pl.ds(block * MAIN, MAIN), :] = tile[:MAIN]
            rests.append(tile[MAIN:])
    for step in range(experts):
        rest = dot(places, jnp.concatenate(rests[step::experts], axis=0))
        out_refs[step][pl.ds(BLOCKS * MAIN, BLOCKS * REST), :] = rest.astype(BF16)


def rest_places(shape, wire, block):
    left = lax.broadcasted_iota(jnp.int32, shape, wire)
    right = lax.broadcasted_iota(jnp.int32, shape, block)
    hit = (lax.rem(right, 16) < REST) & (left == right // 16 * REST + lax.rem(right, 16))
    return hit.astype(F32).astype(BF16)


def in_hbm(array):
    return pltpu.with_memory_space_constraint(array, pltpu.HBM)


def load_kernel(count, *refs):
    sources, targets, sems = refs[:count], refs[count + 2 : 2 * count + 2], refs[-1]
    copies = [
        pltpu.make_async_copy(source, target, sems.at[index])
        for index, (source, target) in enumerate(zip(sources, targets))
    ]
    for copy in copies:
        copy.start()
    for copy in copies:
        copy.wait()


def load(arrays, fragment, after):
    count = len(arrays)
    return pl.pallas_call(
        functools.partial(load_kernel, count),
        out_shape=[pltpu.VMEM(array.shape, array.dtype) for array in arrays],
        in_specs=[HBM] * count + [SMEM, ANY],
        out_specs=[VMEM] * count,
        scratch_shapes=[pltpu.SemaphoreType.DMA((count,))],
        compiler_params=pltpu.CompilerParams(vmem_limit_bytes=8 << 20),
        name="load",
    )(*[in_hbm(array) for array in arrays], fragment, after)


def stack_kernel(*refs):
    *parts, whole = refs
    at = 0
    for part in parts:
        whole[pl.ds(at, part.shape[0]), :] = part[...]
        at += part.shape[0]


def stack(parts):
    rows = sum(part.shape[0] for part in parts)
    return pl.pallas_call(
        stack_kernel,
        out_shape=pltpu.VMEM((rows, parts[0].shape[1]), parts[0].dtype),
        in_specs=[VMEM] * len(parts),
        out_specs=VMEM,
        compiler_params=pltpu.CompilerParams(vmem_limit_bytes=8 << 20),
        name="stack",
    )(*parts)


def pack(experts, tokens, out_grad, ids, weight):
    width = tokens.shape[1]
    inputs = [in_hbm(array) for array in (tokens, out_grad, ids.T, weight.T)]
    return pl.pallas_call(
        functools.partial(pack_kernel, experts),
        out_shape=[pltpu.VMEM((BLOCKS * CAP, width // BLOCKS), BF16)] * experts,
        in_specs=[HBM] * 4,
        out_specs=[VMEM] * experts,
        scratch_shapes=[
            pltpu.VMEM((tokens.shape[0], width), BF16),
            pltpu.VMEM(ids.shape[::-1], jnp.int32),
            pltpu.VMEM(ids.shape[::-1], F32),
            pltpu.SemaphoreType.DMA((3,)),
        ],
        name="pack",
        compiler_params=pltpu.CompilerParams(vmem_limit_bytes=16 << 20),
    )(*inputs)


def join(parts, x_rows, q_rows):
    first = lax.axis_index("tensor") == 0
    cut = x_rows.shape[1] // BLOCKS
    places = rest_places((BLOCKS * 16, BLOCKS * REST), 1, 0)
    row = 0
    for here, there, begin, count in parts:
        for at in range(begin * BLOCKS * CAP, (begin + count) * BLOCKS * CAP, BLOCKS * CAP):
            for block in range(BLOCKS):
                source = pl.ds(at + block * MAIN, MAIN)
                target = (pl.ds(row, MAIN), pl.ds(block * cut, cut))
                x_rows[target] = jnp.where(first, here[source, :], there[source, :])
                q_rows[target] = jnp.where(first, there[source, :], here[source, :])
            source = pl.ds(at + BLOCKS * MAIN, BLOCKS * REST)
            here_rest = dot(places, here[source, :]).astype(BF16)
            there_rest = dot(places, there[source, :]).astype(BF16)
            for block in range(BLOCKS):
                rest = slice(block * 16, block * 16 + 16)
                target = (pl.ds(row + MAIN, 16), pl.ds(block * cut, cut))
                x_rows[target] = jnp.where(first, here_rest[rest], there_rest[rest])
                q_rows[target] = jnp.where(first, there_rest[rest], here_rest[rest])
            row += SLOTS


def activations(x_rows, q_rows, w_gate, w_up, w_down):
    gate_pre = dot(w_gate[...], x_rows[...], 1, 1)
    up_pre = dot(w_up[...], x_rows[...], 1, 1)
    hidden_grad = dot(w_down[...], q_rows[...], 1, 1)
    gate_sig = jax.nn.sigmoid(gate_pre)
    gate_act = gate_pre * gate_sig
    hidden = (gate_act * up_pre).astype(BF16)
    gate_grad = (hidden_grad * up_pre * gate_sig * (1.0 + gate_pre * (1.0 - gate_sig))).astype(BF16)
    up_grad = (hidden_grad * gate_act).astype(BF16)
    return gate_grad, up_grad, hidden


def own_kernel(experts, frag_ref, mine, theirs, w_gate, w_up, w_down, *refs):
    grads, acts, x_rows, q_rows, load_out = refs
    join([(mine, theirs, 0, experts)], x_rows, q_rows)
    for piece, act in enumerate(activations(x_rows, q_rows, w_gate, w_up, w_down)):
        acts[piece] = act
    for piece, rows in enumerate((x_rows, x_rows, q_rows)):
        grads[piece] = dot(acts[piece], rows[...]).astype(BF16)
    total = jnp.zeros((1, 128), F32)
    for step in range(experts):
        full = x_rows[pl.ds(step * SLOTS, SLOTS), pl.ds(0, 128)].astype(F32) < EMPTY / 2
        valid = lax.broadcasted_iota(jnp.int32, full.shape, 0) < CAP
        total += jnp.sum(jnp.where(full & valid, 1.0, 0.0), axis=0, keepdims=True)
    load_out[...] = total / (experts * CAP)


def own(experts, fragment, mine, theirs, weights):
    units, width = weights[0].shape
    rows = experts * SLOTS
    return pl.pallas_call(
        functools.partial(own_kernel, experts),
        out_shape=[
            pltpu.VMEM((3, units, width), BF16),
            pltpu.VMEM((3, units, rows), BF16),
            pltpu.VMEM((rows, width), BF16),
            pltpu.VMEM((rows, width), BF16),
            jax.ShapeDtypeStruct((1, 128), F32),
        ],
        in_specs=[SMEM] + [VMEM] * 5,
        out_specs=[VMEM] * 5,
        name="own",
        compiler_params=pltpu.CompilerParams(vmem_limit_bytes=24 << 20),
        cost_estimate=pl.CostEstimate(
            flops=12 * units * width * rows, bytes_accessed=12 * units * width, transcendentals=0
        ),
    )(fragment, mine, theirs, *weights)


def other_kernel(chunks, frag_ref, mine, theirs, w_gate, w_up, w_down, *refs):
    grads, own_acts, own_x, own_q, *outs, x_rows, q_rows, cuts, sems = refs
    cut = cuts.shape[2]
    frag = frag_ref[0]
    copies = []
    for piece in range(3):
        for step, count in ((1, 2), (2, 1)):
            low, high = (2 * cut, 0) if step == 1 else ((1 - frag) * cut, (5 - frag) * cut)
            begin = jnp.where(frag < 2, low, high)
            columns = pl.ds(pl.multiple_of(begin, cut), count * cut)
            copies.append(
                pltpu.make_async_copy(
                    grads.at[piece, :, columns], outs[piece].at[:, columns], sems.at[piece, step]
                )
            )
            copies[-1].start()
    join([(mine, theirs, 0, chunks)], x_rows, q_rows)
    acts = activations(x_rows, q_rows, w_gate, w_up, w_down)
    columns = pl.ds(pl.multiple_of(frag * cut, cut), cut)
    sides = ((own_x, x_rows), (own_x, x_rows), (own_q, q_rows))
    for piece, (here, there) in enumerate(sides):
        grad = dot(own_acts[piece], here[:, columns]) + dot(acts[piece], there[:, columns])
        cuts[piece] = (grad * 0.5).astype(BF16)
        copies.append(
            pltpu.make_async_copy(cuts.at[piece], outs[piece].at[:, columns], sems.at[piece, 0])
        )
        copies[-1].start()
    for copy in copies:
        copy.wait()


def other(chunks, fragment, mine, theirs, weights, parts):
    units, width = weights[0].shape
    cut = width // FRAGS
    rows = chunks * SLOTS
    return pl.pallas_call(
        functools.partial(other_kernel, chunks),
        out_shape=[jax.ShapeDtypeStruct((units, width), BF16)] * 3,
        in_specs=[SMEM] + [VMEM] * 9,
        out_specs=[HBM] * 3,
        scratch_shapes=[pltpu.VMEM((rows, width), BF16)] * 2
        + [pltpu.VMEM((3, units, cut), BF16), pltpu.SemaphoreType.DMA((3, FRAGS))],
        name="other",
        compiler_params=pltpu.CompilerParams(vmem_limit_bytes=24 << 20),
        cost_estimate=pl.CostEstimate(
            flops=8 * units * width * rows, bytes_accessed=8 * units * width, transcendentals=0
        ),
    )(fragment, mine, theirs, *weights, *parts)


def send(array, axis, step):
    size = lax.axis_size(axis)
    return lax.ppermute(array, axis, [(index, peer(index, step, size)) for index in range(size)])


def tie(*arrays):
    return lax.optimization_barrier(arrays)


def two_replicas(fragment, packed, weights):
    r0 = packed[0]
    r3 = send(packed[3], "expert", 3)
    x0 = send(r0, "replica", 1)
    r1 = send(packed[1], "expert", 1)
    x1 = send(packed[1], ("expert", "replica"), 3)
    r2 = send(packed[2], "expert", 2)
    weights = load(weights, fragment, r0)
    r3, *weights = tie(r3, *weights)
    r2, *weights = tie(r2, *weights)
    x3 = send(r3, "replica", 1)
    x2 = send(r2, "replica", 1)
    r1, x1, x3, x0 = tie(r1, x1, x3, x0)
    near = stack([r0, r1, r2, r3])
    c0 = send(near, "tensor", 1)
    far = stack([x0, x1, x2, x3])
    f0 = send(far, "tensor", 1)
    *parts, filled = own(4, fragment, near, c0, weights)
    grads = other(4, fragment, far, f0, weights, parts)
    return grads, filled


def any_replicas(experts, replicas, fragment, packed, weights):
    mine = [packed[0]] + [send(packed[step], "expert", step) for step in range(1, experts)]
    mine = stack(mine)
    theirs = send(mine, "tensor", 1)
    grads, acts, x_rows, q_rows, filled = own(experts, fragment, mine, theirs, weights)
    cut = x_rows.shape[1] // FRAGS
    begin = fragment[0] * cut
    sides = [lax.dynamic_slice_in_dim(rows, begin, cut, 1) for rows in (x_rows, x_rows, q_rows)]
    pieces = jnp.stack([dot(act, side) for act, side in zip(acts, sides)]).astype(BF16)
    synced = lax.psum(pieces, "replica").astype(F32)
    grads = [
        lax.dynamic_update_slice_in_dim(grad, (piece / replicas).astype(BF16), begin, 1)
        for grad, piece in zip(grads, synced)
    ]
    return grads, filled


def per_device(tokens, out_grad, expert_ids, route_weight, gate_proj, up_proj, down_proj, fragment):
    experts = lax.axis_size("expert")
    replicas = lax.axis_size("replica")
    weights = (gate_proj[0], up_proj[0], down_proj[0])
    packed = pack(experts, tokens[0], out_grad[0], expert_ids[0], route_weight[0])
    if replicas == 2 and experts == 4:
        grads, filled = two_replicas(fragment, packed, weights)
    else:
        grads, filled = any_replicas(experts, replicas, fragment, packed, weights)
    return tuple(grad[None, None] for grad in grads) + (filled[:, :1],)


def solution(mesh):
    rows = P(("group", "replica"), "expert", None)
    units = P("expert", "tensor", None)
    grad = P(("group", "replica"), "expert", "tensor", None)
    return jax.shard_map(
        per_device,
        mesh=mesh,
        in_specs=(rows, rows, rows, rows, units, units, units, P("group")),
        out_specs=(grad, grad, grad, P(("group", "replica"), "expert")),
        check_vma=False,
    )
```

```python
import functools

import jax
import jax.numpy as jnp
from jax import lax
from jax.experimental import pallas as pl
from jax.experimental.pallas import tpu as pltpu
from jax.sharding import PartitionSpec as P

FRAGS = 4
CAP = 60
SLOTS = 64
BLOCKS = 4
MAIN = CAP // 16 * 16
REST = CAP - MAIN
EMPTY = 64.0
F32 = jnp.float32
BF16 = jnp.bfloat16
VMEM = pl.BlockSpec(memory_space=pltpu.VMEM)
SMEM = pl.BlockSpec(memory_space=pltpu.SMEM)
ANY = pl.BlockSpec(memory_space=pl.ANY)
HBM = pl.BlockSpec(memory_space=pltpu.HBM)


def dot(left, right, left_dim=1, right_dim=0):
    return lax.dot_general(
        left, right, (((left_dim,), (right_dim,)), ((), ())), preferred_element_type=F32
    )


def peer(index, step, size):
    return index ^ step if size & (size - 1) == 0 else (index + step) % size


def pack_kernel(experts, tok_hbm, grad_hbm, ids_hbm, weight_hbm, *refs):
    *out_refs, source_ref, ids_ref, weight_ref, sems = refs
    me = lax.axis_index("expert")
    first = lax.axis_index("tensor") == 0
    tokens = ids_ref.shape[1]
    ids_copy = pltpu.make_async_copy(ids_hbm, ids_ref, sems.at[0])
    weight_copy = pltpu.make_async_copy(weight_hbm, weight_ref, sems.at[1])
    ids_copy.start()
    weight_copy.start()
    cut = source_ref.shape[1] // BLOCKS
    tok_copy = pltpu.make_async_copy(tok_hbm, source_ref, sems.at[2])
    grad_copy = pltpu.make_async_copy(grad_hbm, source_ref, sems.at[2])

    @pl.when(first)
    def _():
        tok_copy.start()

    @pl.when(jnp.logical_not(first))
    def _():
        grad_copy.start()

    ids_copy.wait()
    weight_copy.wait()
    ids = ids_ref[...]
    weight = weight_ref[...]
    members, weights = [], []
    for step in range(experts):
        match = ids == peer(me, step, experts)
        members.append(jnp.max(jnp.where(match, 1.0, 0.0), axis=0, keepdims=True))
        weights.append(jnp.sum(jnp.where(match, weight, 0.0), axis=0, keepdims=True))
    member = jnp.concatenate(members, axis=0)
    earlier = (
        lax.broadcasted_iota(jnp.int32, (tokens, tokens), 0)
        < lax.broadcasted_iota(jnp.int32, (tokens, tokens), 1)
    ).astype(F32).astype(BF16)
    position = dot(member.astype(BF16), earlier)
    slot = lax.broadcasted_iota(jnp.int32, (SLOTS, tokens), 0).astype(F32)
    rows = lax.broadcasted_iota(jnp.int32, (SLOTS, 1), 0).astype(F32)
    picks, scales, fills = [], [], []
    for step in range(experts):
        hit = (slot == position[step : step + 1, :]) & (member[step : step + 1, :] > 0.5)
        pick = jnp.where(hit, 1.0, 0.0)
        scale = jnp.sum(pick * weights[step], axis=1, keepdims=True)
        scales.append(jnp.where(first, 1.0, scale))
        count = jnp.sum(members[step], axis=1, keepdims=True)
        fills.append(jnp.where((rows >= count) & first, EMPTY, 0.0))
        picks.append(pick.astype(BF16))
    picks = jnp.concatenate(picks, axis=0)
    scales = jnp.concatenate(scales, axis=0)
    fills = jnp.concatenate(fills, axis=0)
    places = rest_places((BLOCKS * REST, BLOCKS * 16), 0, 1)
    tok_copy.wait()
    packed = (dot(picks, source_ref[...]) * scales + fills).astype(BF16)
    rests = []
    for block in range(BLOCKS):
        for step in range(experts):
            tile = packed[step * SLOTS : (step + 1) * SLOTS, block * cut : (block + 1) * cut]
            out_refs[step][pl.ds(block * MAIN, MAIN), :] = tile[:MAIN]
            rests.append(tile[MAIN:])
    for step in range(experts):
        rest = dot(places, jnp.concatenate(rests[step::experts], axis=0))
        out_refs[step][pl.ds(BLOCKS * MAIN, BLOCKS * REST), :] = rest.astype(BF16)


def rest_places(shape, wire, block):
    left = lax.broadcasted_iota(jnp.int32, shape, wire)
    right = lax.broadcasted_iota(jnp.int32, shape, block)
    hit = (lax.rem(right, 16) < REST) & (left == right // 16 * REST + lax.rem(right, 16))
    return hit.astype(F32).astype(BF16)


def in_hbm(array):
    return pltpu.with_memory_space_constraint(array, pltpu.HBM)


def load_kernel(count, *refs):
    sources, targets, sems = refs[:count], refs[count + 2 : 2 * count + 2], refs[-1]
    copies = [
        pltpu.make_async_copy(source, target, sems.at[index])
        for index, (source, target) in enumerate(zip(sources, targets))
    ]
    for copy in copies:
        copy.start()
    for copy in copies:
        copy.wait()


def load(arrays, fragment, after):
    count = len(arrays)
    return pl.pallas_call(
        functools.partial(load_kernel, count),
        out_shape=[pltpu.VMEM(array.shape, array.dtype) for array in arrays],
        in_specs=[HBM] * count + [SMEM, ANY],
        out_specs=[VMEM] * count,
        scratch_shapes=[pltpu.SemaphoreType.DMA((count,))],
        compiler_params=pltpu.CompilerParams(vmem_limit_bytes=8 << 20),
        name="load",
    )(*[in_hbm(array) for array in arrays], fragment, after)


def stack_kernel(*refs):
    *parts, whole = refs
    at = 0
    for part in parts:
        whole[pl.ds(at, part.shape[0]), :] = part[...]
        at += part.shape[0]


def stack(parts):
    rows = sum(part.shape[0] for part in parts)
    return pl.pallas_call(
        stack_kernel,
        out_shape=pltpu.VMEM((rows, parts[0].shape[1]), parts[0].dtype),
        in_specs=[VMEM] * len(parts),
        out_specs=VMEM,
        compiler_params=pltpu.CompilerParams(vmem_limit_bytes=8 << 20),
        name="stack",
    )(*parts)


def pack(experts, tokens, out_grad, ids, weight):
    width = tokens.shape[1]
    inputs = [in_hbm(array) for array in (tokens, out_grad, ids.T, weight.T)]
    return pl.pallas_call(
        functools.partial(pack_kernel, experts),
        out_shape=[pltpu.VMEM((BLOCKS * CAP, width // BLOCKS), BF16)] * experts,
        in_specs=[HBM] * 4,
        out_specs=[VMEM] * experts,
        scratch_shapes=[
            pltpu.VMEM((tokens.shape[0], width), BF16),
            pltpu.VMEM(ids.shape[::-1], jnp.int32),
            pltpu.VMEM(ids.shape[::-1], F32),
            pltpu.SemaphoreType.DMA((3,)),
        ],
        name="pack",
        compiler_params=pltpu.CompilerParams(vmem_limit_bytes=16 << 20),
    )(*inputs)


def join(parts, x_rows, q_rows):
    first = lax.axis_index("tensor") == 0
    cut = x_rows.shape[1] // BLOCKS
    places = rest_places((BLOCKS * 16, BLOCKS * REST), 1, 0)
    row = 0
    for here, there, begin, count in parts:
        for at in range(begin * BLOCKS * CAP, (begin + count) * BLOCKS * CAP, BLOCKS * CAP):
            for block in range(BLOCKS):
                source = pl.ds(at + block * MAIN, MAIN)
                target = (pl.ds(row, MAIN), pl.ds(block * cut, cut))
                x_rows[target] = jnp.where(first, here[source, :], there[source, :])
                q_rows[target] = jnp.where(first, there[source, :], here[source, :])
            source = pl.ds(at + BLOCKS * MAIN, BLOCKS * REST)
            here_rest = dot(places, here[source, :]).astype(BF16)
            there_rest = dot(places, there[source, :]).astype(BF16)
            for block in range(BLOCKS):
                rest = slice(block * 16, block * 16 + 16)
                target = (pl.ds(row + MAIN, 16), pl.ds(block * cut, cut))
                x_rows[target] = jnp.where(first, here_rest[rest], there_rest[rest])
                q_rows[target] = jnp.where(first, there_rest[rest], here_rest[rest])
            row += SLOTS


def activations(x_rows, q_rows, w_gate, w_up, w_down):
    gate_pre = dot(w_gate[...], x_rows[...], 1, 1)
    up_pre = dot(w_up[...], x_rows[...], 1, 1)
    hidden_grad = dot(w_down[...], q_rows[...], 1, 1)
    gate_sig = jax.nn.sigmoid(gate_pre)
    gate_act = gate_pre * gate_sig
    hidden = (gate_act * up_pre).astype(BF16)
    gate_grad = (hidden_grad * up_pre * gate_sig * (1.0 + gate_pre * (1.0 - gate_sig))).astype(BF16)
    up_grad = (hidden_grad * gate_act).astype(BF16)
    return gate_grad, up_grad, hidden


def own_kernel(experts, frag_ref, mine, theirs, w_gate, w_up, w_down, *refs):
    grads, acts, x_rows, q_rows, load_out = refs
    join([(mine, theirs, 0, experts)], x_rows, q_rows)
    for piece, act in enumerate(activations(x_rows, q_rows, w_gate, w_up, w_down)):
        acts[piece] = act
    for piece, rows in ((2, q_rows), (0, x_rows), (1, x_rows)):
        grads[piece] = dot(acts[piece], rows[...]).astype(BF16)
    total = jnp.zeros((1, 128), F32)
    for step in range(experts):
        full = x_rows[pl.ds(step * SLOTS, SLOTS), pl.ds(0, 128)].astype(F32) < EMPTY / 2
        valid = lax.broadcasted_iota(jnp.int32, full.shape, 0) < CAP
        total += jnp.sum(jnp.where(full & valid, 1.0, 0.0), axis=0, keepdims=True)
    load_out[...] = total / (experts * CAP)


def own(experts, fragment, mine, theirs, weights):
    units, width = weights[0].shape
    rows = experts * SLOTS
    return pl.pallas_call(
        functools.partial(own_kernel, experts),
        out_shape=[
            pltpu.VMEM((3, units, width), BF16),
            pltpu.VMEM((3, units, rows), BF16),
            pltpu.VMEM((rows, width), BF16),
            pltpu.VMEM((rows, width), BF16),
            jax.ShapeDtypeStruct((1, 128), F32),
        ],
        in_specs=[SMEM] + [VMEM] * 5,
        out_specs=[VMEM] * 5,
        name="own",
        compiler_params=pltpu.CompilerParams(vmem_limit_bytes=24 << 20),
        cost_estimate=pl.CostEstimate(
            flops=12 * units * width * rows, bytes_accessed=12 * units * width, transcendentals=0
        ),
    )(fragment, mine, theirs, *weights)


def other_kernel(chunks, frag_ref, mine, theirs, w_gate, w_up, w_down, *refs):
    grads, own_acts, own_x, own_q, *outs, x_rows, q_rows, cuts, sems = refs
    cut = cuts.shape[2]
    frag = frag_ref[0]
    copies = []
    for piece in range(3):
        for step, count in ((1, 2), (2, 1)):
            low, high = (2 * cut, 0) if step == 1 else ((1 - frag) * cut, (5 - frag) * cut)
            begin = jnp.where(frag < 2, low, high)
            columns = pl.ds(pl.multiple_of(begin, cut), count * cut)
            copies.append(
                pltpu.make_async_copy(
                    grads.at[piece, :, columns], outs[piece].at[:, columns], sems.at[piece, step]
                )
            )
            copies[-1].start()
    join([(mine, theirs, 0, chunks)], x_rows, q_rows)
    acts = activations(x_rows, q_rows, w_gate, w_up, w_down)
    columns = pl.ds(pl.multiple_of(frag * cut, cut), cut)
    x_both = jnp.concatenate([own_x[:, columns], x_rows[:, columns]], axis=0)
    q_both = jnp.concatenate([own_q[:, columns], q_rows[:, columns]], axis=0)
    for piece, rows in ((2, q_both), (0, x_both), (1, x_both)):
        grad = dot(jnp.concatenate([own_acts[piece], acts[piece]], axis=1), rows)
        cuts[piece] = (grad * 0.5).astype(BF16)
        copies.append(
            pltpu.make_async_copy(cuts.at[piece], outs[piece].at[:, columns], sems.at[piece, 0])
        )
        copies[-1].start()
    for copy in copies:
        copy.wait()


def other(chunks, fragment, mine, theirs, weights, parts):
    units, width = weights[0].shape
    cut = width // FRAGS
    rows = chunks * SLOTS
    return pl.pallas_call(
        functools.partial(other_kernel, chunks),
        out_shape=[jax.ShapeDtypeStruct((units, width), BF16)] * 3,
        in_specs=[SMEM] + [VMEM] * 9,
        out_specs=[HBM] * 3,
        scratch_shapes=[pltpu.VMEM((rows, width), BF16)] * 2
        + [pltpu.VMEM((3, units, cut), BF16), pltpu.SemaphoreType.DMA((3, FRAGS))],
        name="other",
        compiler_params=pltpu.CompilerParams(vmem_limit_bytes=24 << 20),
        cost_estimate=pl.CostEstimate(
            flops=8 * units * width * rows, bytes_accessed=8 * units * width, transcendentals=0
        ),
    )(fragment, mine, theirs, *weights, *parts)


def send(array, axis, step):
    size = lax.axis_size(axis)
    return lax.ppermute(array, axis, [(index, peer(index, step, size)) for index in range(size)])


def tie(*arrays):
    return lax.optimization_barrier(arrays)


def two_replicas(fragment, packed, weights):
    r0 = packed[0]
    r3 = send(packed[3], "expert", 3)
    x0 = send(r0, "replica", 1)
    r1 = send(packed[1], "expert", 1)
    x1 = send(packed[1], ("expert", "replica"), 3)
    r2 = send(packed[2], "expert", 2)
    weights = load(weights, fragment, r0)
    r3, x0, *weights = tie(r3, x0, *weights)
    r2, *weights = tie(r2, *weights)
    x3 = send(r3, "replica", 1)
    x2 = send(r2, "replica", 1)
    r1, x1, x3 = tie(r1, x1, x3)
    near = stack([r0, r1, r2, r3])
    c0 = send(near, "tensor", 1)
    far = stack([x0, x1, x2, x3])
    f0 = send(far, "tensor", 1)
    *parts, filled = own(4, fragment, near, c0, weights)
    grads = other(4, fragment, far, f0, weights, parts)
    return grads, filled


def any_replicas(experts, replicas, fragment, packed, weights):
    mine = [packed[0]] + [send(packed[step], "expert", step) for step in range(1, experts)]
    mine = stack(mine)
    theirs = send(mine, "tensor", 1)
    grads, acts, x_rows, q_rows, filled = own(experts, fragment, mine, theirs, weights)
    cut = x_rows.shape[1] // FRAGS
    begin = fragment[0] * cut
    sides = [lax.dynamic_slice_in_dim(rows, begin, cut, 1) for rows in (x_rows, x_rows, q_rows)]
    pieces = jnp.stack([dot(act, side) for act, side in zip(acts, sides)]).astype(BF16)
    synced = lax.psum(pieces, "replica").astype(F32)
    grads = [
        lax.dynamic_update_slice_in_dim(grad, (piece / replicas).astype(BF16), begin, 1)
        for grad, piece in zip(grads, synced)
    ]
    return grads, filled


def per_device(tokens, out_grad, expert_ids, route_weight, gate_proj, up_proj, down_proj, fragment):
    experts = lax.axis_size("expert")
    replicas = lax.axis_size("replica")
    weights = (gate_proj[0], up_proj[0], down_proj[0])
    packed = pack(experts, tokens[0], out_grad[0], expert_ids[0], route_weight[0])
    if replicas == 2 and experts == 4:
        grads, filled = two_replicas(fragment, packed, weights)
    else:
        grads, filled = any_replicas(experts, replicas, fragment, packed, weights)
    return tuple(grad[None, None] for grad in grads) + (filled[:, :1],)


def solution(mesh):
    rows = P(("group", "replica"), "expert", None)
    units = P("expert", "tensor", None)
    grad = P(("group", "replica"), "expert", "tensor", None)
    return jax.shard_map(
        per_device,
        mesh=mesh,
        in_specs=(rows, rows, rows, rows, units, units, units, P("group")),
        out_specs=(grad, grad, grad, P(("group", "replica"), "expert")),
        check_vma=False,
    )
```

```python
import functools

import jax
import jax.numpy as jnp
from jax import lax
from jax.experimental import pallas as pl
from jax.experimental.pallas import tpu as pltpu
from jax.sharding import PartitionSpec as P

FRAGS = 4
CAP = 60
SLOTS = 64
BLOCKS = 4
MAIN = CAP // 16 * 16
REST = CAP - MAIN
EMPTY = 64.0
F32 = jnp.float32
BF16 = jnp.bfloat16
VMEM = pl.BlockSpec(memory_space=pltpu.VMEM)
SMEM = pl.BlockSpec(memory_space=pltpu.SMEM)
ANY = pl.BlockSpec(memory_space=pl.ANY)
HBM = pl.BlockSpec(memory_space=pltpu.HBM)


def dot(left, right, left_dim=1, right_dim=0):
    return lax.dot_general(
        left, right, (((left_dim,), (right_dim,)), ((), ())), preferred_element_type=F32
    )


def peer(index, step, size):
    return index ^ step if size & (size - 1) == 0 else (index + step) % size


def pack_kernel(experts, tok_hbm, grad_hbm, ids_hbm, weight_hbm, *refs):
    *out_refs, source_ref, ids_ref, weight_ref, sems = refs
    me = lax.axis_index("expert")
    first = lax.axis_index("tensor") == 0
    tokens = ids_ref.shape[1]
    ids_copy = pltpu.make_async_copy(ids_hbm, ids_ref, sems.at[0])
    weight_copy = pltpu.make_async_copy(weight_hbm, weight_ref, sems.at[1])
    ids_copy.start()
    weight_copy.start()
    cut = source_ref.shape[1] // BLOCKS
    tok_copy = pltpu.make_async_copy(tok_hbm, source_ref, sems.at[2])
    grad_copy = pltpu.make_async_copy(grad_hbm, source_ref, sems.at[2])

    @pl.when(first)
    def _():
        tok_copy.start()

    @pl.when(jnp.logical_not(first))
    def _():
        grad_copy.start()

    ids_copy.wait()
    weight_copy.wait()
    ids = ids_ref[...]
    weight = weight_ref[...]
    members, weights = [], []
    for step in range(experts):
        match = ids == peer(me, step, experts)
        members.append(jnp.max(jnp.where(match, 1.0, 0.0), axis=0, keepdims=True))
        weights.append(jnp.sum(jnp.where(match, weight, 0.0), axis=0, keepdims=True))
    member = jnp.concatenate(members, axis=0)
    earlier = (
        lax.broadcasted_iota(jnp.int32, (tokens, tokens), 0)
        < lax.broadcasted_iota(jnp.int32, (tokens, tokens), 1)
    ).astype(F32).astype(BF16)
    position = dot(member.astype(BF16), earlier)
    row = lax.broadcasted_iota(jnp.int32, (MAIN + BLOCKS * REST, 1), 0)
    block_of = (row - MAIN) // REST
    slot = jnp.where(row < MAIN, row, row - block_of * REST).astype(F32)
    picks, scales, fills = [], [], []
    for step in range(experts):
        hit = (slot == position[step : step + 1, :]) & (member[step : step + 1, :] > 0.5)
        pick = jnp.where(hit, 1.0, 0.0)
        scale = jnp.sum(pick * weights[step], axis=1, keepdims=True)
        scales.append(jnp.where(first, 1.0, scale))
        count = jnp.sum(members[step], axis=1, keepdims=True)
        fills.append(jnp.where((slot >= count) & first, EMPTY, 0.0))
        picks.append(pick.astype(BF16))
    picks = jnp.concatenate(picks, axis=0)
    scales = jnp.concatenate(scales, axis=0)
    fills = jnp.concatenate(fills, axis=0)
    tok_copy.wait()
    packed = dot(picks, source_ref[...]) * scales + fills
    size = MAIN + BLOCKS * REST
    for step in range(experts):
        chunk = packed[step * size : step * size + size]
        rest = chunk[MAIN:, :cut]
        for block in range(BLOCKS):
            columns = slice(block * cut, block * cut + cut)
            out_refs[step][pl.ds(block * MAIN, MAIN), :] = chunk[:MAIN, columns].astype(BF16)
            rest = jnp.where(block_of[MAIN:] == block, chunk[MAIN:, columns], rest)
        out_refs[step][pl.ds(BLOCKS * MAIN, BLOCKS * REST), :] = rest.astype(BF16)


def rest_places(shape, wire, block):
    left = lax.broadcasted_iota(jnp.int32, shape, wire)
    right = lax.broadcasted_iota(jnp.int32, shape, block)
    hit = (lax.rem(right, 16) < REST) & (left == right // 16 * REST + lax.rem(right, 16))
    return hit.astype(F32).astype(BF16)


def in_hbm(array):
    return pltpu.with_memory_space_constraint(array, pltpu.HBM)


def load_kernel(count, *refs):
    sources, targets, sems = refs[:count], refs[count + 2 : 2 * count + 2], refs[-1]
    copies = [
        pltpu.make_async_copy(source, target, sems.at[index])
        for index, (source, target) in enumerate(zip(sources, targets))
    ]
    for copy in copies:
        copy.start()
    for copy in copies:
        copy.wait()


def load(arrays, fragment, after):
    count = len(arrays)
    return pl.pallas_call(
        functools.partial(load_kernel, count),
        out_shape=[pltpu.VMEM(array.shape, array.dtype) for array in arrays],
        in_specs=[HBM] * count + [SMEM, ANY],
        out_specs=[VMEM] * count,
        scratch_shapes=[pltpu.SemaphoreType.DMA((count,))],
        compiler_params=pltpu.CompilerParams(vmem_limit_bytes=8 << 20),
        name="load",
    )(*[in_hbm(array) for array in arrays], fragment, after)


def stack_kernel(*refs):
    *parts, whole = refs
    at = 0
    for part in parts:
        whole[pl.ds(at, part.shape[0]), :] = part[...]
        at += part.shape[0]


def stack(parts):
    rows = sum(part.shape[0] for part in parts)
    return pl.pallas_call(
        stack_kernel,
        out_shape=pltpu.VMEM((rows, parts[0].shape[1]), parts[0].dtype),
        in_specs=[VMEM] * len(parts),
        out_specs=VMEM,
        compiler_params=pltpu.CompilerParams(vmem_limit_bytes=8 << 20),
        name="stack",
    )(*parts)


def pack(experts, tokens, out_grad, ids, weight):
    width = tokens.shape[1]
    inputs = [in_hbm(array) for array in (tokens, out_grad, ids.T, weight.T)]
    return pl.pallas_call(
        functools.partial(pack_kernel, experts),
        out_shape=[pltpu.VMEM((BLOCKS * CAP, width // BLOCKS), BF16)] * experts,
        in_specs=[HBM] * 4,
        out_specs=[VMEM] * experts,
        scratch_shapes=[
            pltpu.VMEM((tokens.shape[0], width), BF16),
            pltpu.VMEM(ids.shape[::-1], jnp.int32),
            pltpu.VMEM(ids.shape[::-1], F32),
            pltpu.SemaphoreType.DMA((3,)),
        ],
        name="pack",
        compiler_params=pltpu.CompilerParams(vmem_limit_bytes=16 << 20),
    )(*inputs)


def join(parts, x_rows, q_rows):
    first = lax.axis_index("tensor") == 0
    cut = x_rows.shape[1] // BLOCKS
    places = rest_places((BLOCKS * 16, BLOCKS * REST), 1, 0)
    row = 0
    for here, there, begin, count in parts:
        for at in range(begin * BLOCKS * CAP, (begin + count) * BLOCKS * CAP, BLOCKS * CAP):
            for block in range(BLOCKS):
                source = pl.ds(at + block * MAIN, MAIN)
                target = (pl.ds(row, MAIN), pl.ds(block * cut, cut))
                x_rows[target] = jnp.where(first, here[source, :], there[source, :])
                q_rows[target] = jnp.where(first, there[source, :], here[source, :])
            source = pl.ds(at + BLOCKS * MAIN, BLOCKS * REST)
            here_rest = dot(places, here[source, :]).astype(BF16)
            there_rest = dot(places, there[source, :]).astype(BF16)
            for block in range(BLOCKS):
                rest = slice(block * 16, block * 16 + 16)
                target = (pl.ds(row + MAIN, 16), pl.ds(block * cut, cut))
                x_rows[target] = jnp.where(first, here_rest[rest], there_rest[rest])
                q_rows[target] = jnp.where(first, there_rest[rest], here_rest[rest])
            row += SLOTS


def activations(x_rows, q_rows, w_gate, w_up, w_down):
    gate_pre = dot(w_gate[...], x_rows[...], 1, 1)
    up_pre = dot(w_up[...], x_rows[...], 1, 1)
    gate_sig = jax.nn.sigmoid(gate_pre)
    gate_act = gate_pre * gate_sig
    hidden = (gate_act * up_pre).astype(BF16)
    hidden_grad = dot(w_down[...], q_rows[...], 1, 1)
    up_grad = (hidden_grad * gate_act).astype(BF16)
    gate_grad = (hidden_grad * up_pre * gate_sig * (1.0 + gate_pre * (1.0 - gate_sig))).astype(BF16)
    return gate_grad, up_grad, hidden


def own_kernel(experts, frag_ref, mine, theirs, w_gate, w_up, w_down, *refs):
    grads, acts, x_rows, q_rows, load_out = refs
    join([(mine, theirs, 0, experts)], x_rows, q_rows)
    for piece, act in enumerate(activations(x_rows, q_rows, w_gate, w_up, w_down)):
        acts[piece] = act
    for piece, rows in ((2, q_rows), (1, x_rows), (0, x_rows)):
        grads[piece] = dot(acts[piece], rows[...]).astype(BF16)
    total = jnp.zeros((1, 128), F32)
    for step in range(experts):
        full = x_rows[pl.ds(step * SLOTS, SLOTS), pl.ds(0, 128)].astype(F32) < EMPTY / 2
        valid = lax.broadcasted_iota(jnp.int32, full.shape, 0) < CAP
        total += jnp.sum(jnp.where(full & valid, 1.0, 0.0), axis=0, keepdims=True)
    load_out[...] = total / (experts * CAP)


def own(experts, fragment, mine, theirs, weights):
    units, width = weights[0].shape
    rows = experts * SLOTS
    return pl.pallas_call(
        functools.partial(own_kernel, experts),
        out_shape=[
            pltpu.VMEM((3, units, width), BF16),
            pltpu.VMEM((3, units, rows), BF16),
            pltpu.VMEM((rows, width), BF16),
            pltpu.VMEM((rows, width), BF16),
            jax.ShapeDtypeStruct((1, 128), F32),
        ],
        in_specs=[SMEM] + [VMEM] * 5,
        out_specs=[VMEM] * 5,
        name="own",
        compiler_params=pltpu.CompilerParams(vmem_limit_bytes=24 << 20),
        cost_estimate=pl.CostEstimate(
            flops=12 * units * width * rows, bytes_accessed=12 * units * width, transcendentals=0
        ),
    )(fragment, mine, theirs, *weights)


def other_kernel(chunks, frag_ref, mine, theirs, w_gate, w_up, w_down, *refs):
    grads, own_acts, own_x, own_q, *outs, x_rows, q_rows, cuts, sems = refs
    cut = cuts.shape[2]
    frag = frag_ref[0]
    copies = []
    for piece in range(3):
        for step, count in ((1, 2), (2, 1)):
            low, high = (2 * cut, 0) if step == 1 else ((1 - frag) * cut, (5 - frag) * cut)
            begin = jnp.where(frag < 2, low, high)
            columns = pl.ds(pl.multiple_of(begin, cut), count * cut)
            copies.append(
                pltpu.make_async_copy(
                    grads.at[piece, :, columns], outs[piece].at[:, columns], sems.at[piece, step]
                )
            )
            copies[-1].start()
    join([(mine, theirs, 0, chunks)], x_rows, q_rows)
    acts = activations(x_rows, q_rows, w_gate, w_up, w_down)
    columns = pl.ds(pl.multiple_of(frag * cut, cut), cut)
    x_both = jnp.concatenate([own_x[:, columns], x_rows[:, columns]], axis=0)
    q_both = jnp.concatenate([own_q[:, columns], q_rows[:, columns]], axis=0)
    for piece, rows in ((2, q_both), (0, x_both), (1, x_both)):
        grad = dot(jnp.concatenate([own_acts[piece], acts[piece]], axis=1), rows)
        cuts[piece] = (grad * 0.5).astype(BF16)
        copies.append(
            pltpu.make_async_copy(cuts.at[piece], outs[piece].at[:, columns], sems.at[piece, 0])
        )
        copies[-1].start()
    for copy in copies:
        copy.wait()


def other(chunks, fragment, mine, theirs, weights, parts):
    units, width = weights[0].shape
    cut = width // FRAGS
    rows = chunks * SLOTS
    return pl.pallas_call(
        functools.partial(other_kernel, chunks),
        out_shape=[jax.ShapeDtypeStruct((units, width), BF16)] * 3,
        in_specs=[SMEM] + [VMEM] * 9,
        out_specs=[HBM] * 3,
        scratch_shapes=[pltpu.VMEM((rows, width), BF16)] * 2
        + [pltpu.VMEM((3, units, cut), BF16), pltpu.SemaphoreType.DMA((3, FRAGS))],
        name="other",
        compiler_params=pltpu.CompilerParams(vmem_limit_bytes=24 << 20),
        cost_estimate=pl.CostEstimate(
            flops=8 * units * width * rows, bytes_accessed=8 * units * width, transcendentals=0
        ),
    )(fragment, mine, theirs, *weights, *parts)


def send(array, axis, step):
    size = lax.axis_size(axis)
    return lax.ppermute(array, axis, [(index, peer(index, step, size)) for index in range(size)])


def tie(*arrays):
    return lax.optimization_barrier(arrays)


def two_replicas(fragment, packed, weights):
    r0 = packed[0]
    r3 = send(packed[3], "expert", 3)
    x0 = send(r0, "replica", 1)
    r1 = send(packed[1], "expert", 1)
    x1 = send(packed[1], ("expert", "replica"), 3)
    r2 = send(packed[2], "expert", 2)
    weights = load(weights, fragment, r0)
    r3, x0, *weights = tie(r3, x0, *weights)
    r2, r0 = tie(r2, r0)
    x3 = send(r3, "replica", 1)
    x2 = send(r2, "replica", 1)
    r1, x1, x3 = tie(r1, x1, x3)
    near = stack([r0, r1, r2, r3])
    c0 = send(near, "tensor", 1)
    far = stack([x0, x1, x2, x3])
    f0 = send(far, "tensor", 1)
    *parts, filled = own(4, fragment, near, c0, weights)
    grads = other(4, fragment, far, f0, weights, parts)
    return grads, filled


def any_replicas(experts, replicas, fragment, packed, weights):
    mine = [packed[0]] + [send(packed[step], "expert", step) for step in range(1, experts)]
    mine = stack(mine)
    theirs = send(mine, "tensor", 1)
    grads, acts, x_rows, q_rows, filled = own(experts, fragment, mine, theirs, weights)
    cut = x_rows.shape[1] // FRAGS
    begin = fragment[0] * cut
    sides = [lax.dynamic_slice_in_dim(rows, begin, cut, 1) for rows in (x_rows, x_rows, q_rows)]
    pieces = jnp.stack([dot(act, side) for act, side in zip(acts, sides)]).astype(BF16)
    synced = lax.psum(pieces, "replica").astype(F32)
    grads = [
        lax.dynamic_update_slice_in_dim(grad, (piece / replicas).astype(BF16), begin, 1)
        for grad, piece in zip(grads, synced)
    ]
    return grads, filled


def per_device(tokens, out_grad, expert_ids, route_weight, gate_proj, up_proj, down_proj, fragment):
    experts = lax.axis_size("expert")
    replicas = lax.axis_size("replica")
    weights = (gate_proj[0], up_proj[0], down_proj[0])
    packed = pack(experts, tokens[0], out_grad[0], expert_ids[0], route_weight[0])
    if replicas == 2 and experts == 4:
        grads, filled = two_replicas(fragment, packed, weights)
    else:
        grads, filled = any_replicas(experts, replicas, fragment, packed, weights)
    return tuple(grad[None, None] for grad in grads) + (filled[:, :1],)


def solution(mesh):
    rows = P(("group", "replica"), "expert", None)
    units = P("expert", "tensor", None)
    grad = P(("group", "replica"), "expert", "tensor", None)
    return jax.shard_map(
        per_device,
        mesh=mesh,
        in_specs=(rows, rows, rows, rows, units, units, units, P("group")),
        out_specs=(grad, grad, grad, P(("group", "replica"), "expert")),
        check_vma=False,
    )
```

```python
import functools

import jax
import jax.numpy as jnp
from jax import lax
from jax.experimental import pallas as pl
from jax.experimental.pallas import tpu as pltpu
from jax.sharding import PartitionSpec as P

FRAGS = 4
CAP = 60
SLOTS = 64
BLOCKS = 4
MAIN = CAP // 16 * 16
REST = CAP - MAIN
EMPTY = 64.0
F32 = jnp.float32
BF16 = jnp.bfloat16
VMEM = pl.BlockSpec(memory_space=pltpu.VMEM)
SMEM = pl.BlockSpec(memory_space=pltpu.SMEM)
ANY = pl.BlockSpec(memory_space=pl.ANY)
HBM = pl.BlockSpec(memory_space=pltpu.HBM)


def dot(left, right, left_dim=1, right_dim=0):
    return lax.dot_general(
        left, right, (((left_dim,), (right_dim,)), ((), ())), preferred_element_type=F32
    )


def peer(index, step, size):
    return index ^ step if size & (size - 1) == 0 else (index + step) % size


def pack_kernel(experts, tok_hbm, grad_hbm, ids_hbm, weight_hbm, *refs):
    *out_refs, source_ref, ids_ref, weight_ref, sems = refs
    me = lax.axis_index("expert")
    first = lax.axis_index("tensor") == 0
    tokens = ids_ref.shape[1]
    ids_copy = pltpu.make_async_copy(ids_hbm, ids_ref, sems.at[0])
    weight_copy = pltpu.make_async_copy(weight_hbm, weight_ref, sems.at[1])
    ids_copy.start()
    weight_copy.start()
    cut = source_ref.shape[1] // BLOCKS
    tok_copy = pltpu.make_async_copy(tok_hbm, source_ref, sems.at[2])
    grad_copy = pltpu.make_async_copy(grad_hbm, source_ref, sems.at[2])

    @pl.when(first)
    def _():
        tok_copy.start()

    @pl.when(jnp.logical_not(first))
    def _():
        grad_copy.start()

    ids_copy.wait()
    weight_copy.wait()
    ids = ids_ref[...]
    weight = weight_ref[...]
    members, weights = [], []
    for step in range(experts):
        match = ids == peer(me, step, experts)
        members.append(jnp.max(jnp.where(match, 1.0, 0.0), axis=0, keepdims=True))
        weights.append(jnp.sum(jnp.where(match, weight, 0.0), axis=0, keepdims=True))
    member = jnp.concatenate(members, axis=0)
    earlier = (
        lax.broadcasted_iota(jnp.int32, (tokens, tokens), 0)
        < lax.broadcasted_iota(jnp.int32, (tokens, tokens), 1)
    ).astype(F32).astype(BF16)
    position = dot(member.astype(BF16), earlier)
    row = lax.broadcasted_iota(jnp.int32, (MAIN + BLOCKS * REST, 1), 0)
    block_of = (row - MAIN) // REST
    slot = jnp.where(row < MAIN, row, row - block_of * REST).astype(F32)
    picks, scales, fills = [], [], []
    for step in range(experts):
        hit = (slot == position[step : step + 1, :]) & (member[step : step + 1, :] > 0.5)
        pick = jnp.where(hit, 1.0, 0.0)
        scale = jnp.sum(pick * weights[step], axis=1, keepdims=True)
        scales.append(jnp.where(first, 1.0, scale))
        count = jnp.sum(members[step], axis=1, keepdims=True)
        fills.append(jnp.where((slot >= count) & first, EMPTY, 0.0))
        picks.append(pick.astype(BF16))
    picks = jnp.concatenate(picks, axis=0)
    scales = jnp.concatenate(scales, axis=0)
    fills = jnp.concatenate(fills, axis=0)
    tok_copy.wait()
    packed = dot(picks, source_ref[...]) * scales + fills
    size = MAIN + BLOCKS * REST
    for step in range(experts):
        chunk = packed[step * size : step * size + size]
        rest = chunk[MAIN:, :cut]
        for block in range(BLOCKS):
            columns = slice(block * cut, block * cut + cut)
            out_refs[step][pl.ds(block * MAIN, MAIN), :] = chunk[:MAIN, columns].astype(BF16)
            rest = jnp.where(block_of[MAIN:] == block, chunk[MAIN:, columns], rest)
        out_refs[step][pl.ds(BLOCKS * MAIN, BLOCKS * REST), :] = rest.astype(BF16)


def rest_places(shape, wire, block):
    left = lax.broadcasted_iota(jnp.int32, shape, wire)
    right = lax.broadcasted_iota(jnp.int32, shape, block)
    hit = (lax.rem(right, 16) < REST) & (left == right // 16 * REST + lax.rem(right, 16))
    return hit.astype(F32).astype(BF16)


def in_hbm(array):
    return pltpu.with_memory_space_constraint(array, pltpu.HBM)


def load_kernel(count, *refs):
    sources, targets, sems = refs[:count], refs[count + 2 : 2 * count + 2], refs[-1]
    copies = [
        pltpu.make_async_copy(source, target, sems.at[index])
        for index, (source, target) in enumerate(zip(sources, targets))
    ]
    for copy in copies:
        copy.start()
    for copy in copies:
        copy.wait()


def load(arrays, fragment, after):
    count = len(arrays)
    return pl.pallas_call(
        functools.partial(load_kernel, count),
        out_shape=[pltpu.VMEM(array.shape, array.dtype) for array in arrays],
        in_specs=[HBM] * count + [SMEM, ANY],
        out_specs=[VMEM] * count,
        scratch_shapes=[pltpu.SemaphoreType.DMA((count,))],
        compiler_params=pltpu.CompilerParams(vmem_limit_bytes=8 << 20),
        name="load",
    )(*[in_hbm(array) for array in arrays], fragment, after)


def stack_kernel(*refs):
    *parts, whole = refs
    at = 0
    for part in parts:
        whole[pl.ds(at, part.shape[0]), :] = part[...]
        at += part.shape[0]


def stack(parts):
    rows = sum(part.shape[0] for part in parts)
    return pl.pallas_call(
        stack_kernel,
        out_shape=pltpu.VMEM((rows, parts[0].shape[1]), parts[0].dtype),
        in_specs=[VMEM] * len(parts),
        out_specs=VMEM,
        compiler_params=pltpu.CompilerParams(vmem_limit_bytes=8 << 20),
        name="stack",
    )(*parts)


def pack(experts, tokens, out_grad, ids, weight):
    width = tokens.shape[1]
    inputs = [in_hbm(array) for array in (tokens, out_grad, ids.T, weight.T)]
    return pl.pallas_call(
        functools.partial(pack_kernel, experts),
        out_shape=[pltpu.VMEM((BLOCKS * CAP, width // BLOCKS), BF16)] * experts,
        in_specs=[HBM] * 4,
        out_specs=[VMEM] * experts,
        scratch_shapes=[
            pltpu.VMEM((tokens.shape[0], width), BF16),
            pltpu.VMEM(ids.shape[::-1], jnp.int32),
            pltpu.VMEM(ids.shape[::-1], F32),
            pltpu.SemaphoreType.DMA((3,)),
        ],
        name="pack",
        compiler_params=pltpu.CompilerParams(vmem_limit_bytes=16 << 20),
    )(*inputs)


def join(parts, x_rows, q_rows):
    first = lax.axis_index("tensor") == 0
    cut = x_rows.shape[1] // BLOCKS
    places = rest_places((BLOCKS * 16, BLOCKS * REST), 1, 0)
    row = 0
    for here, there, begin, count in parts:
        for at in range(begin * BLOCKS * CAP, (begin + count) * BLOCKS * CAP, BLOCKS * CAP):
            for block in range(BLOCKS):
                source = pl.ds(at + block * MAIN, MAIN)
                target = (pl.ds(row, MAIN), pl.ds(block * cut, cut))
                x_rows[target] = jnp.where(first, here[source, :], there[source, :])
                q_rows[target] = jnp.where(first, there[source, :], here[source, :])
            source = pl.ds(at + BLOCKS * MAIN, BLOCKS * REST)
            here_rest = dot(places, here[source, :]).astype(BF16)
            there_rest = dot(places, there[source, :]).astype(BF16)
            for block in range(BLOCKS):
                rest = slice(block * 16, block * 16 + 16)
                target = (pl.ds(row + MAIN, 16), pl.ds(block * cut, cut))
                x_rows[target] = jnp.where(first, here_rest[rest], there_rest[rest])
                q_rows[target] = jnp.where(first, there_rest[rest], here_rest[rest])
            row += SLOTS


def activations(x_rows, q_rows, w_gate, w_up, w_down):
    gate_pre = dot(w_gate[...], x_rows[...], 1, 1)
    up_pre = dot(w_up[...], x_rows[...], 1, 1)
    gate_sig = jax.nn.sigmoid(gate_pre)
    gate_act = gate_pre * gate_sig
    hidden = (gate_act * up_pre).astype(BF16)
    hidden_grad = dot(w_down[...], q_rows[...], 1, 1)
    up_grad = (hidden_grad * gate_act).astype(BF16)
    gate_grad = (hidden_grad * up_pre * gate_sig * (1.0 + gate_pre * (1.0 - gate_sig))).astype(BF16)
    return gate_grad, up_grad, hidden


def own_kernel(experts, frag_ref, mine, theirs, w_gate, w_up, w_down, *refs):
    grads, sums, load_out, acts, x_rows, q_rows = refs
    join([(mine, theirs, 0, experts)], x_rows, q_rows)
    for piece, act in enumerate(activations(x_rows, q_rows, w_gate, w_up, w_down)):
        acts[piece] = act
    cut = sums.shape[2]
    frag_columns = pl.ds(pl.multiple_of(frag_ref[0] * cut, cut), cut)
    for piece, rows in ((2, q_rows), (1, x_rows), (0, x_rows)):
        grads[piece] = dot(acts[piece], rows[...]).astype(BF16)
        sums[piece] = dot(acts[piece], rows[:, frag_columns])
    total = jnp.zeros((1, 128), F32)
    for step in range(experts):
        full = x_rows[pl.ds(step * SLOTS, SLOTS), pl.ds(0, 128)].astype(F32) < EMPTY / 2
        valid = lax.broadcasted_iota(jnp.int32, full.shape, 0) < CAP
        total += jnp.sum(jnp.where(full & valid, 1.0, 0.0), axis=0, keepdims=True)
    load_out[...] = total / (experts * CAP)


def own(experts, fragment, mine, theirs, weights):
    units, width = weights[0].shape
    rows = experts * SLOTS
    return pl.pallas_call(
        functools.partial(own_kernel, experts),
        out_shape=[
            pltpu.VMEM((3, units, width), BF16),
            pltpu.VMEM((3, units, width // FRAGS), F32),
            jax.ShapeDtypeStruct((1, 128), F32),
        ],
        in_specs=[SMEM] + [VMEM] * 5,
        out_specs=[VMEM] * 3,
        scratch_shapes=[pltpu.VMEM((3, units, rows), BF16)] + [pltpu.VMEM((rows, width), BF16)] * 2,
        name="own",
        compiler_params=pltpu.CompilerParams(vmem_limit_bytes=24 << 20),
        cost_estimate=pl.CostEstimate(
            flops=12 * units * width * rows, bytes_accessed=12 * units * width, transcendentals=0
        ),
    )(fragment, mine, theirs, *weights)


def other_kernel(chunks, frag_ref, mine, theirs, w_gate, w_up, w_down, *refs):
    grads, sums, *outs, x_rows, q_rows, cuts, sems = refs
    cut = cuts.shape[2]
    frag = frag_ref[0]
    copies = []
    for piece in range(3):
        for step, count in ((1, 2), (2, 1)):
            low, high = (2 * cut, 0) if step == 1 else ((1 - frag) * cut, (5 - frag) * cut)
            begin = jnp.where(frag < 2, low, high)
            columns = pl.ds(pl.multiple_of(begin, cut), count * cut)
            copies.append(
                pltpu.make_async_copy(
                    grads.at[piece, :, columns], outs[piece].at[:, columns], sems.at[piece, step]
                )
            )
            copies[-1].start()
    join([(mine, theirs, 0, chunks)], x_rows, q_rows)
    acts = activations(x_rows, q_rows, w_gate, w_up, w_down)
    columns = pl.ds(pl.multiple_of(frag * cut, cut), cut)
    for piece, rows in ((2, q_rows), (0, x_rows), (1, x_rows)):
        grad = sums[piece] + dot(acts[piece], rows[:, columns])
        cuts[piece] = (grad * 0.5).astype(BF16)
        copies.append(
            pltpu.make_async_copy(cuts.at[piece], outs[piece].at[:, columns], sems.at[piece, 0])
        )
        copies[-1].start()
    for copy in copies:
        copy.wait()


def other(chunks, fragment, mine, theirs, weights, parts):
    units, width = weights[0].shape
    cut = width // FRAGS
    rows = chunks * SLOTS
    return pl.pallas_call(
        functools.partial(other_kernel, chunks),
        out_shape=[jax.ShapeDtypeStruct((units, width), BF16)] * 3,
        in_specs=[SMEM] + [VMEM] * 7,
        out_specs=[HBM] * 3,
        scratch_shapes=[pltpu.VMEM((rows, width), BF16)] * 2
        + [pltpu.VMEM((3, units, cut), BF16), pltpu.SemaphoreType.DMA((3, FRAGS))],
        name="other",
        compiler_params=pltpu.CompilerParams(vmem_limit_bytes=24 << 20),
        cost_estimate=pl.CostEstimate(
            flops=8 * units * width * rows, bytes_accessed=8 * units * width, transcendentals=0
        ),
    )(fragment, mine, theirs, *weights, *parts)


def send(array, axis, step):
    size = lax.axis_size(axis)
    return lax.ppermute(array, axis, [(index, peer(index, step, size)) for index in range(size)])


def tie(*arrays):
    return lax.optimization_barrier(arrays)


def two_replicas(fragment, packed, weights):
    r0 = packed[0]
    r3 = send(packed[3], "expert", 3)
    x0 = send(r0, "replica", 1)
    r1 = send(packed[1], "expert", 1)
    x1 = send(packed[1], ("expert", "replica"), 3)
    r2 = send(packed[2], "expert", 2)
    weights = load(weights, fragment, r0)
    r3, x0, *weights = tie(r3, x0, *weights)
    r2, r0 = tie(r2, r0)
    x3 = send(r3, "replica", 1)
    x2 = send(r2, "replica", 1)
    r1, x1, x3 = tie(r1, x1, x3)
    near = stack([r0, r1, r2, r3])
    c0 = send(near, "tensor", 1)
    far = stack([x0, x1, x2, x3])
    f0 = send(far, "tensor", 1)
    *parts, filled = own(4, fragment, near, c0, weights)
    grads = other(4, fragment, far, f0, weights, parts)
    return grads, filled


def any_replicas(experts, replicas, fragment, packed, weights):
    mine = [packed[0]] + [send(packed[step], "expert", step) for step in range(1, experts)]
    mine = stack(mine)
    theirs = send(mine, "tensor", 1)
    grads, sums, filled = own(experts, fragment, mine, theirs, weights)
    begin = fragment[0] * sums.shape[2]
    synced = lax.psum(sums.astype(BF16), "replica").astype(F32)
    grads = [
        lax.dynamic_update_slice_in_dim(grad, (piece / replicas).astype(BF16), begin, 1)
        for grad, piece in zip(grads, synced)
    ]
    return grads, filled


def per_device(tokens, out_grad, expert_ids, route_weight, gate_proj, up_proj, down_proj, fragment):
    experts = lax.axis_size("expert")
    replicas = lax.axis_size("replica")
    weights = (gate_proj[0], up_proj[0], down_proj[0])
    packed = pack(experts, tokens[0], out_grad[0], expert_ids[0], route_weight[0])
    if replicas == 2 and experts == 4:
        grads, filled = two_replicas(fragment, packed, weights)
    else:
        grads, filled = any_replicas(experts, replicas, fragment, packed, weights)
    return tuple(grad[None, None] for grad in grads) + (filled[:, :1],)


def solution(mesh):
    rows = P(("group", "replica"), "expert", None)
    units = P("expert", "tensor", None)
    grad = P(("group", "replica"), "expert", "tensor", None)
    return jax.shard_map(
        per_device,
        mesh=mesh,
        in_specs=(rows, rows, rows, rows, units, units, units, P("group")),
        out_specs=(grad, grad, grad, P(("group", "replica"), "expert")),
        check_vma=False,
    )
```
